32 devices in a mesh: parts: 2 (over y), az: 16 (over z, x, core).
Axes of the slice: x: 2, y: 2, z: 4, core: 2. Of those that a mesh axis runs over, the one named last changes fastest.
Arguments:
- fields: bfloat16 [256, 64, 128], P(('parts', 'az')), parts along dimension 0, may hold values from -6 to 6
- cotangent: bfloat16 [256, 64, 128], P(('parts', 'az')), parts along dimension 0, may hold values from -21 to 21
- azimuth_filter: float32 [9, 64], replicated, may hold values from -2 to 2
- radial_filter: float32 [7, 64], replicated, may hold values from -2 to 2
- mixing: bfloat16 [64, 64], replicated, may hold values from -0.75 to 0.75
- tap_offsets: int32 [9], replicated, may hold values from -48 to 48, as said below
Outputs:
- output_field: bfloat16 [256, 64, 128], P(('parts', 'az')), parts along dimension 0
- input_grad: bfloat16 [256, 64, 128], P(('parts', 'az')), parts along dimension 0
- azimuth_grad: float32 [18, 64], P('parts'), parts along dimension 0
- radial_grad: float32 [14, 64], P('parts'), parts along dimension 0
- mixing_grad: float32 [128, 64], P('parts'), parts along dimension 0
The draws below stay inside these ranges and needn't reach their ends.
There are 2 independent parts, one for each index of `parts`. The reference program is written for one: setup_inputs(seed, part) draws one part's arguments, and reference() takes and returns one part's arrays. A program takes and returns all parts, laid end to end along the dimension named above; an argument that names none is the same for every part. Nothing has to cross between parts.
Inputs may be any that keep to these rules, and one draw needn't show every extreme that they name: `tap_offsets`: offsets are distinct and rise with the tap; the first is the most negative and the last the most positive.
All inputs are finite; a program needn't handle non-finite values.
Results may differ from the reference program's by a relative error of at most 0.008.
Values may be sent and summed in bfloat16 or wider, within the bound.
No kernel may reach another device: no remote copies, remote signals or barrier semaphores. Data moves between devices by JAX's collectives and lax.ppermute only.
A program may use at most 64 MiB of HBM per device.

```python
import math
import jax
import jax.numpy as jnp
from jax import lax

C = 64
TAPS = 9
RTAPS = 7
AXIAL = 2
AZIM = 128
RAD = 64
FEAT = 128


def draw_tap_offsets(key, part):
    key = jax.random.fold_in(key, 11)
    stride = AZIM // 10
    spread = stride // 4
    jitter = jax.random.randint(key, (TAPS,), -spread, spread + 1)
    positions = jnp.arange(TAPS, dtype=jnp.int32)
    ends = (positions == 0) | (positions == TAPS - 1)
    jitter = jnp.where(ends, 0, jitter)
    return ((positions - TAPS // 2) * stride + jitter).astype(jnp.int32)


def draw_cotangent(key, part):
    key = jax.random.fold_in(key, 23)
    first = jax.random.fold_in(key, 0)
    ramp = jnp.exp(math.log(3.0) * jnp.arange(AZIM, dtype=jnp.float32) / (AZIM - 1))[:, None, None]
    value = jnp.clip(jax.random.normal(first, (AZIM, RAD, FEAT), jnp.float32), -4.0, 4.0) * ramp
    return value.astype(jnp.bfloat16)


def steps_of(key, dims, shards, smallest, top_value):
    factor_of, own = 1.0, jax.random.fold_in(key, 6)
    for axis_at, blocks in shards:
        heights = jnp.exp(jax.random.uniform(jax.random.fold_in(own, axis_at), (blocks,), jnp.float32, smallest / len(shards), top_value / len(shards)))
        factor_of = factor_of * jnp.repeat(heights, dims[axis_at] // blocks).reshape([-1 if axis == axis_at else 1 for axis in range(len(dims))])
    return factor_of


def scatter_about(key, dims, scale, limit, cuts=(), kind=jnp.bfloat16):
    array = jax.random.normal(key, dims, jnp.float32) * scale
    if len(cuts) > 0:
        array = steps_of(key, dims, cuts, -0.22, 0.18) * array
    return jnp.clip(array, min=-limit, max=limit).astype(kind)


def setup_inputs(seed: int = 0, part: int = 0) -> dict:
    arg_keys = jax.random.split(jax.random.key(seed), 7)
    part_splits = jax.random.split(jax.random.fold_in(arg_keys[6], part), 7)
    return {
        "fields": scatter_about(part_splits[0], (AZIM, RAD, FEAT), 1.0, 6.0, ((0, 16),)),
        "cotangent": draw_cotangent(jax.random.fold_in(jax.random.fold_in(arg_keys[6], part), 71), part),
        "azimuth_filter": scatter_about(arg_keys[2], (TAPS, C), TAPS ** -0.5, 2.0, (), jnp.float32),
        "radial_filter": scatter_about(arg_keys[3], (RTAPS, C), RTAPS ** -0.5, 2.0, (), jnp.float32),
        "mixing": scatter_about(arg_keys[4], (C, C), C ** -0.5, 0.75),
        "tap_offsets": draw_tap_offsets(jax.random.fold_in(arg_keys[6], 71), part),
    }


def one_slab(fields, cotangent, azimuth_filter, radial_filter, mixing, tap_offsets, axial_index):
    start = axial_index * C
    field_part = lax.dynamic_slice_in_dim(fields, start, C, 2)
    cot_part = lax.dynamic_slice_in_dim(cotangent, start, C, 2)
    field_float = field_part.astype(jnp.float32)
    azim_sum = jnp.zeros((AZIM, RAD, C), jnp.float32)
    for tap in range(TAPS):
        azim_sum = azim_sum + azimuth_filter[tap] * jnp.roll(field_float, -tap_offsets[tap], axis=0)
    azim_padded = jnp.pad(azim_sum, ((0, 0), (3, 3), (0, 0)))
    radial_sum = jnp.zeros((AZIM, RAD, C), jnp.float32)
    for tap in range(RTAPS):
        radial_sum = radial_sum + radial_filter[tap] * azim_padded[:, tap:tap + RAD]
    hidden = radial_sum.astype(jnp.bfloat16)
    hidden_flat = hidden.reshape(-1, C)
    cot_flat = cot_part.reshape(-1, C)
    mixed = jnp.dot(hidden_flat, mixing, preferred_element_type=jnp.float32).reshape(AZIM, RAD, C)
    output_part = (field_float + mixed).astype(jnp.bfloat16)
    grad_hidden = jnp.dot(cot_flat, mixing.T, preferred_element_type=jnp.float32).astype(jnp.bfloat16)
    mix_term = jnp.dot(hidden_flat.T, cot_flat, preferred_element_type=jnp.float32)
    grad_float = grad_hidden.reshape(AZIM, RAD, C).astype(jnp.float32)
    grad_padded = jnp.pad(grad_float, ((0, 0), (3, 3), (0, 0)))
    grad_azim = jnp.zeros((AZIM, RAD, C), jnp.float32)
    radial_terms = []
    for tap in range(RTAPS):
        grad_azim = grad_azim + radial_filter[tap] * grad_padded[:, 6 - tap:6 - tap + RAD]
        radial_terms.append(jnp.sum(azim_padded[:, tap:tap + RAD] * grad_float, axis=(0, 1)))
    branch = jnp.zeros((AZIM, RAD, C), jnp.float32)
    azim_terms = []
    for tap in range(TAPS):
        shifted = jnp.roll(field_float, -tap_offsets[tap], axis=0)
        azim_terms.append(jnp.sum(shifted * grad_azim, axis=(0, 1)))
        branch = branch + azimuth_filter[tap] * jnp.roll(grad_azim, tap_offsets[tap], axis=0)
    branch_grad = lax.optimization_barrier(branch.astype(jnp.bfloat16))
    input_part = (cot_part.astype(jnp.float32) + branch_grad.astype(jnp.float32)).astype(jnp.bfloat16)
    return output_part, input_part, jnp.stack(azim_terms), jnp.stack(radial_terms), mix_term


def reference(fields, cotangent, azimuth_filter, radial_filter, mixing, tap_offsets):
    def step(axial_index):
        return one_slab(fields, cotangent, azimuth_filter, radial_filter, mixing, tap_offsets, axial_index)

    outputs, inputs, azim_terms, radial_terms, mix_terms = lax.map(step, jnp.arange(AXIAL, dtype=jnp.int32))
    scale = 1.0 / (float(AZIM * RAD * AXIAL) ** 0.5)
    output_field = jnp.transpose(outputs, (1, 2, 0, 3)).reshape(AZIM, RAD, FEAT)
    input_grad = jnp.transpose(inputs, (1, 2, 0, 3)).reshape(AZIM, RAD, FEAT)
    azimuth_grad = scale * jnp.sum(azim_terms, axis=0)
    radial_grad = scale * jnp.sum(radial_terms, axis=0)
    mixing_grad = scale * jnp.sum(mix_terms, axis=0)
    return output_field, input_grad, azimuth_grad, radial_grad, mixing_grad
```

```python
import functools
import math

import jax
import jax.numpy as jnp
from jax import lax
from jax.experimental import pallas as pl
from jax.experimental.pallas import tpu as pltpu
from jax.sharding import PartitionSpec as P

F32, BF16 = jnp.float32, jnp.bfloat16
VMEM = pl.BlockSpec(memory_space=pltpu.VMEM)
SMEM = pl.BlockSpec(memory_space=pltpu.SMEM)
ROWS = 8
HALO = 3
SLAB = 8
PARAMS = pltpu.CompilerParams(vmem_limit_bytes=56 * 1024 * 1024)


def place():
    at = lax.axis_index("az")
    return at // 2, at % 2


def widen(azimuth_ref, radial_ref, mixing_ref, filters_ref, mix_ref):
    taps, channels = azimuth_ref.shape
    rtaps = radial_ref.shape[0]
    feat = mix_ref.shape[0]
    filters_ref[...] = jnp.zeros(filters_ref.shape, F32)
    mix_ref[...] = jnp.zeros(mix_ref.shape, BF16)
    for low in range(0, feat, channels):
        cell = slice(low, low + channels)
        filters_ref[0:taps, cell] = azimuth_ref[...]
        filters_ref[taps : taps + rtaps, cell] = radial_ref[...]
        mix_ref[cell, cell] = mixing_ref[...]


def visit(refs, stage, step, fill=False):
    if stage is None:
        for i, ref in enumerate(refs):
            step(i, ref)
        return
    if not fill:
        for i, ref in enumerate(refs):
            stage[i] = ref[...]

    def body(i, carry):
        step(i, stage.at[i])
        return carry

    lax.fori_loop(0, len(refs), body, 0)
    if fill:
        for i, ref in enumerate(refs):
            ref[...] = stage[i]


def partner(rounds, i, side):
    return 2 * (rounds - 1 - i) + side


def pack(rounds, own_f, own_g, other_f, other_g, *refs):
    outs, (fields, cots, *stage) = refs[:rounds], refs[rounds:]
    chip, core = place()
    near, rad, feat = own_f.shape
    step = rad + 2 * ROWS
    wide = fields.reshape(2 * near, step, feat)
    edge = jnp.zeros((2 * near, ROWS, feat), F32)
    wide[:, 0:ROWS, :] = edge
    wide[:, ROWS + rad : step, :] = edge
    for side, f, g in ((core, own_f, own_g), (1 - core, other_f, other_g)):
        wide[pl.ds(side * near, near), ROWS : ROWS + rad, :] = f[...].astype(F32)
        cots[pl.ds(side * near, near)] = g[...].astype(F32)
    body = 2 * near * ROWS

    def step_(i, out):
        to = chip ^ partner(rounds, i, core)
        first = pl.multiple_of(to * ROWS, ROWS)
        center = wide[:, pl.ds(pl.multiple_of(first + ROWS, ROWS), ROWS), :]
        out[0:body, :] = center.reshape(body, feat).astype(BF16)
        for h in range(2 * HALO):
            row = first + ROWS + (h - HALO if h < HALO else ROWS + h - HALO)
            at = body + h * 2 * near
            out[at : at + 2 * near, :] = fields[pl.ds(row, 2 * near, stride=step), :].astype(BF16)
        at = body + 2 * HALO * 2 * near
        out[at : at + body, :] = cots[:, pl.ds(first, ROWS), :].reshape(body, feat).astype(BF16)

    visit(outs, stage[0] if stage else None, step_, fill=True)


def convolve(rounds, taps, rtaps, channels, offsets, filters, mix, *refs):
    blocks, outs = refs[: 2 * rounds], refs[2 * rounds : 3 * rounds]
    fields, radial, grads, cots, hidden, spread, *stage = refs[3 * rounds :]
    chip, core = place()
    azim = radial.shape[0] // 2
    feat = mix.shape[0]
    step = 2 * ROWS
    wide = fields.reshape(azim, step, feat)
    near = azim // (2 * rounds)
    body = near * ROWS
    weight = [jnp.broadcast_to(filters[k : k + 1, :], (ROWS, feat)) for k in range(taps + rtaps)]
    def take(side, i, block):
        source = chip ^ partner(rounds, i, side)
        first = source * near
        wide[pl.ds(first, near), HALO : HALO + ROWS, :] = (
            block[0:body, :].astype(F32).reshape(near, ROWS, feat)
        )
        for h in range(2 * HALO):
            row = h if h < HALO else ROWS + h
            at = body + h * near
            fields[pl.ds(first * step + row, near, stride=step), :] = block[
                at : at + near, :
            ].astype(F32)
        at = body + 2 * HALO * near
        cot = block[at : at + body, :]
        cots[pl.ds(pl.multiple_of(first * ROWS, body), body), :] = cot
        back = lax.dot_general(cot, mix[...], (((1,), (1,)), ((), ())), preferred_element_type=F32)
        back = back.astype(BF16).astype(F32).reshape(near, ROWS, feat)
        grads[pl.ds(first, near)] = back
        grads[pl.ds(azim + first, near)] = back
        total = weight[taps] * wide[pl.ds(first, near), 0:ROWS, :]
        for j in range(1, rtaps):
            total = total + weight[taps + j] * wide[pl.ds(first, near), j : j + ROWS, :]
        radial[pl.ds(first, near)] = total
        radial[pl.ds(azim + first, near)] = total
    for side, group in ((core, blocks[:rounds]), (1 - core, blocks[rounds:])):
        visit(group, stage[0] if stage else None, functools.partial(take, side))
    ahead = [lax.rem(offsets[k] + azim, azim) for k in range(taps)]
    behind = [lax.rem(azim - offsets[k], azim) for k in range(taps)]

    def slab(n, sums):
        sums = list(sums)
        a = n * SLAB
        grad = grads[pl.ds(a, SLAB)]
        value = jnp.zeros((SLAB, ROWS, feat), F32)
        back = jnp.zeros((SLAB, ROWS, feat), F32)
        for k in range(taps):
            x = radial[pl.ds(a + ahead[k], SLAB)]
            value = value + weight[k] * x
            sums[k] = sums[k] + jnp.sum(x * grad, axis=0)
            back = back + weight[k] * grads[pl.ds(a + behind[k], SLAB)]
        rows = pl.ds(pl.multiple_of(a * ROWS, SLAB * ROWS), SLAB * ROWS)
        hidden[rows, :] = value.reshape(SLAB * ROWS, feat).astype(BF16)
        spread[rows, :] = back.reshape(SLAB * ROWS, feat).astype(BF16)
        for j in range(rtaps):
            sums[taps + j] = sums[taps + j] + jnp.sum(
                wide[pl.ds(a, SLAB), j : j + ROWS, :] * back, axis=0
            )
        return tuple(sums)

    zero = jnp.zeros((ROWS, feat), F32)
    sums = lax.fori_loop(0, azim // SLAB, slab, (zero,) * (taps + rtaps))
    product = lax.dot_general(
        hidden[...], cots[...], (((0,), (0,)), ((), ())), preferred_element_type=F32
    )
    lane = lax.broadcasted_iota(jnp.int32, (channels, feat), 1)
    mixed = jnp.where(lane < channels, product[0:channels], product[channels:feat])
    part = jnp.concatenate([jnp.sum(s, axis=0, keepdims=True) for s in sums] + [mixed], axis=0)
    part = part + pltpu.roll(part, channels, 1)
    few, half = (taps + rtaps) // 2, channels // 2
    low = jnp.concatenate([part[0:few], part[2 * few : 2 * few + half]], axis=0)
    high = jnp.concatenate([part[few : 2 * few], part[2 * few + half : 2 * few + channels]], axis=0)
    lane = lax.broadcasted_iota(jnp.int32, low.shape, 1)
    part = jnp.where(lane < channels, low, high)
    part = jnp.concatenate([part, jnp.zeros((8, feat), F32)], axis=0).astype(BF16)
    for i, out in enumerate(outs):
        to = chip ^ partner(rounds, i, core)
        rows = pl.ds(pl.multiple_of(to * body, body), body)
        out[0:body, :] = hidden[rows, :]
        out[body : 2 * body, :] = spread[rows, :]
        out[2 * body : 2 * body + part.shape[0], :] = part


def finish(rounds, taps, rtaps, scale, field, cot, filters, mix, *refs):
    blocks = refs[: 2 * rounds]
    out, grad, azimuth_out, radial_out, mixing_out, hidden, spread, summed, *stage = refs[2 * rounds :]
    chip, core = place()
    near, rad, feat = field.shape
    channels = azimuth_out.shape[1]
    body = near * ROWS
    spread[:, 0:ROWS, :] = jnp.zeros((near, ROWS, feat), F32)
    spread[:, ROWS + rad :, :] = jnp.zeros((near, ROWS, feat), F32)
    few, half = (taps + rtaps) // 2, channels // 2
    mine = pl.multiple_of(core * body, body)
    summed[...] = jnp.zeros(summed.shape, F32)

    def take(side, i, block):
        first = pl.multiple_of((chip ^ partner(rounds, i, side)) * ROWS, ROWS)
        hidden[:, pl.ds(first, ROWS), :] = (
            block[pl.ds(mine, body), :].astype(F32).reshape(near, ROWS, feat)
        )
        spread[:, pl.ds(pl.multiple_of(first + ROWS, ROWS), ROWS), :] = (
            block[pl.ds(2 * body + mine, body), :].astype(F32).reshape(near, ROWS, feat)
        )
        summed[...] += block[4 * body : 4 * body + summed.shape[0], :].astype(F32)

    for side, group in ((core, blocks[:rounds]), (1 - core, blocks[rounds:])):
        visit(group, stage[0] if stage else None, functools.partial(take, side))
    part = summed[0 : few + half, :] * scale
    azimuth_out[0:few, :] = part[0:few, 0:channels]
    azimuth_out[few:taps, :] = part[0 : taps - few, channels:feat]
    radial_out[...] = part[taps - few : few, channels:feat]
    mixing_out[0:half, :] = part[few : few + half, 0:channels]
    mixing_out[half:channels, :] = part[few : few + half, channels:feat]
    flat = hidden[...].reshape(near * rad, feat).astype(BF16)
    mixed = jnp.dot(flat, mix[...], preferred_element_type=F32).reshape(near, rad, feat)
    out[...] = (field[...].astype(F32) + mixed).astype(BF16)
    total = jnp.zeros((near, rad, feat), F32)
    for j in range(rtaps):
        weight = jnp.broadcast_to(filters[taps + j : taps + j + 1, :], (rad, feat))
        first = ROWS + HALO - j
        total = total + weight * spread[:, first : first + rad, :]
    branch = total.astype(BF16).astype(F32)
    grad[...] = (cot[...].astype(F32) + branch).astype(BF16)


def call(kernel, ins, outs, scratch, keep=False, name=None):
    ins = [pltpu.with_memory_space_constraint(x, pltpu.VMEM) if x.ndim > 1 else x for x in ins]
    return pl.pallas_call(
        kernel,
        in_specs=[VMEM if x.ndim > 1 else SMEM for x in ins],
        out_specs=[VMEM] * len(outs),
        out_shape=[(pltpu.VMEM if keep else jax.ShapeDtypeStruct)(*out) for out in outs],
        scratch_shapes=[pltpu.VMEM(*out) for out in scratch],
        compiler_params=PARAMS,
        name=name,
    )(*ins)


def swap(x):
    size = lax.axis_size("az")
    return lax.ppermute(x, "az", [(i, i ^ 1) for i in range(size)])


def exchange(messages):
    chips = lax.axis_size("az") // 2
    got = []
    for i, message in enumerate(messages):
        pairs = [
            (2 * c + k, 2 * (c ^ partner(len(messages), i, k)) + k) for c in range(chips) for k in range(2)
        ]
        got.append(lax.ppermute(message, "az", pairs))
    return got + [swap(x) for x in got]


def local(fields, cotangent, azimuth_filter, radial_filter, mixing, tap_offsets):
    size = lax.axis_size("az")
    rounds = size // 4
    near, rad, feat = fields.shape
    azim = near * size
    taps, rtaps, channels = tap_offsets.shape[0], radial_filter.shape[0], mixing.shape[0]
    many = rounds > 8
    other_f, other_g = swap(fields), swap(cotangent)
    filters, mix = call(
        widen,
        (azimuth_filter, radial_filter, mixing),
        [((taps + rtaps, feat), F32), ((feat, feat), BF16)],
        [],
        keep=True,
        name="widen",
    )
    other_f, other_g, filters, mix = lax.optimization_barrier((other_f, other_g, filters, mix))
    body = 2 * near * ROWS
    length = 2 * body + 2 * HALO * 2 * near
    message = ((length, feat), BF16)
    messages = call(
        functools.partial(pack, rounds),
        (fields, cotangent, other_f, other_g),
        [message] * rounds,
        [((2 * near * (rad + 2 * ROWS), feat), F32), ((2 * near, rad, feat), F32)]
        + [((rounds, length, feat), BF16)] * many,
        keep=True,
        name="pack",
    )
    blocks = exchange(messages)
    sums = (taps + rtaps + channels) // 2 + 8
    flat = ((azim * ROWS, feat), BF16)
    messages = call(
        functools.partial(convolve, rounds, taps, rtaps, channels),
        (tap_offsets, filters, mix, *blocks),
        [((2 * body + sums, feat), BF16)] * rounds,
        [((azim * 2 * ROWS, feat), F32)]
        + [((2 * azim, ROWS, feat), F32)] * 2
        + [flat] * 3
        + [((rounds, length, feat), BF16)] * many,
        keep=True,
        name="convolve",
    )
    blocks = exchange(messages)
    scale = 1.0 / math.sqrt(azim * rad * (feat // channels))
    return call(
        functools.partial(finish, rounds, taps, rtaps, scale),
        (fields, cotangent, filters, mix, *blocks),
        [
            (fields.shape, BF16),
            (fields.shape, BF16),
            ((taps, channels), F32),
            ((rtaps, channels), F32),
            ((channels, channels), F32),
        ],
        [((near, rad, feat), F32), ((near, rad + 2 * ROWS, feat), F32), ((sums, feat), F32)]
        + [((rounds, 2 * body + sums, feat), BF16)] * many,
        name="finish",
    )


def solution(mesh):
    cells = P(("parts", "az"), None, None)
    parts = P("parts", None)
    return jax.shard_map(
        lambda *args: tuple(local(*args)),
        mesh=mesh,
        in_specs=(cells, cells, P(), P(), P(), P()),
        out_specs=(cells, cells, parts, parts, parts),
        check_vma=False,
    )
```

```python
import functools
import math

import jax
import jax.numpy as jnp
from jax import lax
from jax.experimental import pallas as pl
from jax.experimental.pallas import tpu as pltpu
from jax.sharding import PartitionSpec as P

F32, BF16 = jnp.float32, jnp.bfloat16
VMEM = pl.BlockSpec(memory_space=pltpu.VMEM)
SMEM = pl.BlockSpec(memory_space=pltpu.SMEM)
ROWS = 8
HALO = 3
SLAB = 8
PARAMS = pltpu.CompilerParams(vmem_limit_bytes=56 * 1024 * 1024)


def place():
    at = lax.axis_index("az")
    return at // 2, at % 2


def gather(field, cot, azimuth, radial, mixing, offsets, *refs):
    own_f, own_g, filters, mix, own_offsets, azimuth_in, radial_in, mixing_in, sems = refs
    pairs = (
        (azimuth, azimuth_in),
        (radial, radial_in),
        (mixing, mixing_in),
        (offsets, own_offsets),
        (field, own_f),
        (cot, own_g),
    )
    copies = [pltpu.make_async_copy(*pair, sems.at[i]) for i, pair in enumerate(pairs)]
    for copy in copies:
        copy.start()
    filters[...] = jnp.zeros(filters.shape, F32)
    mix[...] = jnp.zeros(mix.shape, BF16)
    for copy in copies[:3]:
        copy.wait()
    taps, channels = azimuth_in.shape
    rtaps, feat = radial_in.shape[0], mix.shape[0]
    for low in range(0, feat, channels):
        cell = slice(low, low + channels)
        filters[0:taps, cell] = azimuth_in[...]
        filters[taps : taps + rtaps, cell] = radial_in[...]
        mix[cell, cell] = mixing_in[...]
    for copy in copies[3:]:
        copy.wait()


def visit(refs, stage, step, fill=False):
    if stage is None:
        for i, ref in enumerate(refs):
            step(i, ref)
        return
    if not fill:
        for i, ref in enumerate(refs):
            stage[i] = ref[...]

    def body(i, carry):
        step(i, stage.at[i])
        return carry

    lax.fori_loop(0, len(refs), body, 0)
    if fill:
        for i, ref in enumerate(refs):
            ref[...] = stage[i]


def partner(rounds, i, side):
    return 2 * (rounds - 1 - i) + side


def pack(rounds, own_f, own_g, other_f, other_g, *refs):
    outs, (fields, cots, *stage) = refs[:rounds], refs[rounds:]
    chip, core = place()
    near, rad, feat = own_f.shape
    step = rad + 2 * ROWS
    wide = fields.reshape(2 * near, step, feat)
    edge = jnp.zeros((2 * near, ROWS, feat), F32)
    wide[:, 0:ROWS, :] = edge
    wide[:, ROWS + rad : step, :] = edge
    for side, f, g in ((core, own_f, own_g), (1 - core, other_f, other_g)):
        wide[pl.ds(side * near, near), ROWS : ROWS + rad, :] = f[...].astype(F32)
        cots[pl.ds(side * near, near)] = g[...].astype(F32)
    body = 2 * near * ROWS

    def step_(i, out):
        to = chip ^ partner(rounds, i, core)
        first = pl.multiple_of(to * ROWS, ROWS)
        center = wide[:, pl.ds(pl.multiple_of(first + ROWS, ROWS), ROWS), :]
        out[0:body, :] = center.reshape(body, feat).astype(BF16)
        for h in range(2 * HALO):
            row = first + ROWS + (h - HALO if h < HALO else ROWS + h - HALO)
            at = body + h * 2 * near
            out[at : at + 2 * near, :] = fields[pl.ds(row, 2 * near, stride=step), :].astype(BF16)
        at = body + 2 * HALO * 2 * near
        out[at : at + body, :] = cots[:, pl.ds(first, ROWS), :].reshape(body, feat).astype(BF16)

    visit(outs, stage[0] if stage else None, step_, fill=True)


def convolve(rounds, taps, rtaps, channels, offsets, filters, mix, *refs):
    blocks, outs = refs[: 2 * rounds], refs[2 * rounds : 3 * rounds]
    fields, radial, grads, cots, hidden, spread, *stage = refs[3 * rounds :]
    chip, core = place()
    azim = radial.shape[0] // 2
    feat = mix.shape[0]
    step = 2 * ROWS
    wide = fields.reshape(azim, step, feat)
    near = azim // (2 * rounds)
    body = near * ROWS
    weight = [jnp.broadcast_to(filters[k : k + 1, :], (ROWS, feat)) for k in range(taps + rtaps)]
    def take(side, i, block):
        source = chip ^ partner(rounds, i, side)
        first = source * near
        wide[pl.ds(first, near), HALO : HALO + ROWS, :] = (
            block[0:body, :].astype(F32).reshape(near, ROWS, feat)
        )
        for h in range(2 * HALO):
            row = h if h < HALO else ROWS + h
            at = body + h * near
            fields[pl.ds(first * step + row, near, stride=step), :] = block[
                at : at + near, :
            ].astype(F32)
        at = body + 2 * HALO * near
        cot = block[at : at + body, :]
        cots[pl.ds(pl.multiple_of(first * ROWS, body), body), :] = cot
        back = lax.dot_general(cot, mix[...], (((1,), (1,)), ((), ())), preferred_element_type=F32)
        back = back.astype(BF16).astype(F32).reshape(near, ROWS, feat)
        grads[pl.ds(first, near)] = back
        grads[pl.ds(azim + first, near)] = back
        total = weight[taps] * wide[pl.ds(first, near), 0:ROWS, :]
        for j in range(1, rtaps):
            total = total + weight[taps + j] * wide[pl.ds(first, near), j : j + ROWS, :]
        radial[pl.ds(first, near)] = total
        radial[pl.ds(azim + first, near)] = total
    for side, group in ((core, blocks[:rounds]), (1 - core, blocks[rounds:])):
        visit(group, stage[0] if stage else None, functools.partial(take, side))
    ahead = [lax.rem(offsets[k] + azim, azim) for k in range(taps)]
    behind = [lax.rem(azim - offsets[k], azim) for k in range(taps)]

    def slab(n, sums):
        sums = list(sums)
        a = n * SLAB
        grad = grads[pl.ds(a, SLAB)]
        value = jnp.zeros((SLAB, ROWS, feat), F32)
        back = jnp.zeros((SLAB, ROWS, feat), F32)
        for k in range(taps):
            x = radial[pl.ds(a + ahead[k], SLAB)]
            value = value + weight[k] * x
            sums[k] = sums[k] + jnp.sum(x * grad, axis=0)
            back = back + weight[k] * grads[pl.ds(a + behind[k], SLAB)]
        rows = pl.ds(pl.multiple_of(a * ROWS, SLAB * ROWS), SLAB * ROWS)
        hidden[rows, :] = value.reshape(SLAB * ROWS, feat).astype(BF16)
        spread[rows, :] = back.reshape(SLAB * ROWS, feat).astype(BF16)
        for j in range(rtaps):
            sums[taps + j] = sums[taps + j] + jnp.sum(
                wide[pl.ds(a, SLAB), j : j + ROWS, :] * back, axis=0
            )
        return tuple(sums)

    zero = jnp.zeros((ROWS, feat), F32)
    sums = lax.fori_loop(0, azim // SLAB, slab, (zero,) * (taps + rtaps))
    product = lax.dot_general(
        hidden[...], cots[...], (((0,), (0,)), ((), ())), preferred_element_type=F32
    )
    lane = lax.broadcasted_iota(jnp.int32, (channels, feat), 1)
    mixed = jnp.where(lane < channels, product[0:channels], product[channels:feat])
    part = jnp.concatenate([jnp.sum(s, axis=0, keepdims=True) for s in sums] + [mixed], axis=0)
    part = part + pltpu.roll(part, channels, 1)
    few, half = (taps + rtaps) // 2, channels // 2
    low = jnp.concatenate([part[0:few], part[2 * few : 2 * few + half]], axis=0)
    high = jnp.concatenate([part[few : 2 * few], part[2 * few + half : 2 * few + channels]], axis=0)
    lane = lax.broadcasted_iota(jnp.int32, low.shape, 1)
    part = jnp.where(lane < channels, low, high)
    part = jnp.concatenate([part, jnp.zeros((8, feat), F32)], axis=0).astype(BF16)
    for i, out in enumerate(outs):
        to = chip ^ partner(rounds, i, core)
        rows = pl.ds(pl.multiple_of(to * body, body), body)
        out[0:body, :] = hidden[rows, :]
        out[body : 2 * body, :] = spread[rows, :]
        out[2 * body : 2 * body + part.shape[0], :] = part


def finish(rounds, taps, rtaps, scale, field, cot, filters, mix, *refs):
    blocks = refs[: 2 * rounds]
    out, grad, azimuth_out, radial_out, mixing_out, hidden, spread, summed, *stage = refs[2 * rounds :]
    chip, core = place()
    near, rad, feat = field.shape
    channels = azimuth_out.shape[1]
    body = near * ROWS
    spread[:, 0:ROWS, :] = jnp.zeros((near, ROWS, feat), F32)
    spread[:, ROWS + rad :, :] = jnp.zeros((near, ROWS, feat), F32)
    few, half = (taps + rtaps) // 2, channels // 2
    mine = pl.multiple_of(core * body, body)
    summed[...] = jnp.zeros(summed.shape, F32)

    def take(side, i, block):
        first = pl.multiple_of((chip ^ partner(rounds, i, side)) * ROWS, ROWS)
        hidden[:, pl.ds(first, ROWS), :] = (
            block[pl.ds(mine, body), :].astype(F32).reshape(near, ROWS, feat)
        )
        spread[:, pl.ds(pl.multiple_of(first + ROWS, ROWS), ROWS), :] = (
            block[pl.ds(2 * body + mine, body), :].astype(F32).reshape(near, ROWS, feat)
        )
        summed[...] += block[4 * body : 4 * body + summed.shape[0], :].astype(F32)

    for side, group in ((core, blocks[:rounds]), (1 - core, blocks[rounds:])):
        visit(group, stage[0] if stage else None, functools.partial(take, side))
    part = summed[0 : few + half, :] * scale
    azimuth_out[0:few, :] = part[0:few, 0:channels]
    azimuth_out[few:taps, :] = part[0 : taps - few, channels:feat]
    radial_out[...] = part[taps - few : few, channels:feat]
    mixing_out[0:half, :] = part[few : few + half, 0:channels]
    mixing_out[half:channels, :] = part[few : few + half, channels:feat]
    flat = hidden[...].reshape(near * rad, feat).astype(BF16)
    mixed = jnp.dot(flat, mix[...], preferred_element_type=F32).reshape(near, rad, feat)
    out[...] = (field[...].astype(F32) + mixed).astype(BF16)
    total = jnp.zeros((near, rad, feat), F32)
    for j in range(rtaps):
        weight = jnp.broadcast_to(filters[taps + j : taps + j + 1, :], (rad, feat))
        first = ROWS + HALO - j
        total = total + weight * spread[:, first : first + rad, :]
    branch = total.astype(BF16).astype(F32)
    grad[...] = (cot[...].astype(F32) + branch).astype(BF16)


def call(kernel, ins, outs, scratch, keep=False, name=None):
    ins = [
        pltpu.with_memory_space_constraint(x, pltpu.VMEM if x.ndim > 1 else pltpu.SMEM) for x in ins
    ]
    return pl.pallas_call(
        kernel,
        in_specs=[VMEM if x.ndim > 1 else SMEM for x in ins],
        out_specs=[VMEM] * len(outs),
        out_shape=[(pltpu.VMEM if keep else jax.ShapeDtypeStruct)(*out) for out in outs],
        scratch_shapes=[pltpu.VMEM(*out) for out in scratch],
        compiler_params=PARAMS,
        name=name,
    )(*ins)


def swap(x):
    size = lax.axis_size("az")
    return lax.ppermute(x, "az", [(i, i ^ 1) for i in range(size)])


def exchange(messages):
    chips = lax.axis_size("az") // 2
    got = []
    for i, message in enumerate(messages):
        pairs = [
            (2 * c + k, 2 * (c ^ partner(len(messages), i, k)) + k) for c in range(chips) for k in range(2)
        ]
        got.append(lax.ppermute(message, "az", pairs))
    return got + [swap(x) for x in got]


def local(fields, cotangent, azimuth_filter, radial_filter, mixing, tap_offsets):
    size = lax.axis_size("az")
    rounds = size // 4
    near, rad, feat = fields.shape
    azim = near * size
    taps, rtaps, channels = tap_offsets.shape[0], radial_filter.shape[0], mixing.shape[0]
    many = rounds > 8
    other_f, other_g = swap(fields), swap(cotangent)
    arguments = (fields, cotangent, azimuth_filter, radial_filter, mixing, tap_offsets)
    kept = [
        pltpu.VMEM(fields.shape, BF16),
        pltpu.VMEM(fields.shape, BF16),
        pltpu.VMEM((taps + rtaps, feat), F32),
        pltpu.VMEM((feat, feat), BF16),
        pltpu.SMEM((taps,), jnp.int32),
    ]
    fields, cotangent, filters, mix, tap_offsets = pl.pallas_call(
        gather,
        in_specs=[pl.BlockSpec(memory_space=pltpu.HBM)] * len(arguments),
        out_specs=[VMEM] * 4 + [SMEM],
        out_shape=kept,
        scratch_shapes=[
            pltpu.VMEM(azimuth_filter.shape, F32),
            pltpu.VMEM(radial_filter.shape, F32),
            pltpu.VMEM(mixing.shape, BF16),
            pltpu.SemaphoreType.DMA((len(arguments),)),
        ],
        compiler_params=PARAMS,
        name="gather",
    )(*(pltpu.with_memory_space_constraint(x, pltpu.HBM) for x in arguments))
    other_f, other_g, fields, cotangent = lax.optimization_barrier(
        (other_f, other_g, fields, cotangent)
    )
    body = 2 * near * ROWS
    length = 2 * body + 2 * HALO * 2 * near
    message = ((length, feat), BF16)
    messages = call(
        functools.partial(pack, rounds),
        (fields, cotangent, other_f, other_g),
        [message] * rounds,
        [((2 * near * (rad + 2 * ROWS), feat), F32), ((2 * near, rad, feat), F32)]
        + [((rounds, length, feat), BF16)] * many,
        keep=True,
        name="pack",
    )
    blocks = exchange(messages)
    sums = (taps + rtaps + channels) // 2 + 8
    flat = ((azim * ROWS, feat), BF16)
    messages = call(
        functools.partial(convolve, rounds, taps, rtaps, channels),
        (tap_offsets, filters, mix, *blocks),
        [((2 * body + sums, feat), BF16)] * rounds,
        [((azim * 2 * ROWS, feat), F32)]
        + [((2 * azim, ROWS, feat), F32)] * 2
        + [flat] * 3
        + [((rounds, length, feat), BF16)] * many,
        keep=True,
        name="convolve",
    )
    blocks = exchange(messages)
    scale = 1.0 / math.sqrt(azim * rad * (feat // channels))
    return call(
        functools.partial(finish, rounds, taps, rtaps, scale),
        (fields, cotangent, filters, mix, *blocks),
        [
            (fields.shape, BF16),
            (fields.shape, BF16),
            ((taps, channels), F32),
            ((rtaps, channels), F32),
            ((channels, channels), F32),
        ],
        [((near, rad, feat), F32), ((near, rad + 2 * ROWS, feat), F32), ((sums, feat), F32)]
        + [((rounds, 2 * body + sums, feat), BF16)] * many,
        name="finish",
    )


def solution(mesh):
    cells = P(("parts", "az"), None, None)
    parts = P("parts", None)
    return jax.shard_map(
        lambda *args: tuple(local(*args)),
        mesh=mesh,
        in_specs=(cells, cells, P(), P(), P(), P()),
        out_specs=(cells, cells, parts, parts, parts),
        check_vma=False,
    )
```

```python
import functools
import math

import jax
import jax.numpy as jnp
from jax import lax
from jax.experimental import pallas as pl
from jax.experimental.pallas import tpu as pltpu
from jax.sharding import PartitionSpec as P

F32, BF16 = jnp.float32, jnp.bfloat16
VMEM = pl.BlockSpec(memory_space=pltpu.VMEM)
SMEM = pl.BlockSpec(memory_space=pltpu.SMEM)
ROWS = 8
HALO = 3
SLAB = 8
PARAMS = pltpu.CompilerParams(vmem_limit_bytes=56 * 1024 * 1024)


def place():
    at = lax.axis_index("az")
    return at // 2, at % 2


def gather(field, cot, azimuth, radial, mixing, offsets, *refs):
    own_f, own_g, filters, mix, own_offsets, azimuth_in, radial_in, mixing_in, sems = refs
    pairs = (
        (azimuth, azimuth_in),
        (radial, radial_in),
        (mixing, mixing_in),
        (offsets, own_offsets),
        (field, own_f),
        (cot, own_g),
    )
    copies = [pltpu.make_async_copy(*pair, sems.at[i]) for i, pair in enumerate(pairs)]
    for copy in copies:
        copy.start()
    filters[...] = jnp.zeros(filters.shape, F32)
    mix[...] = jnp.zeros(mix.shape, BF16)
    for copy in copies[:3]:
        copy.wait()
    taps, channels = azimuth_in.shape
    rtaps, feat = radial_in.shape[0], mix.shape[0]
    for low in range(0, feat, channels):
        cell = slice(low, low + channels)
        filters[0:taps, cell] = azimuth_in[...]
        filters[taps : taps + rtaps, cell] = radial_in[...]
        mix[cell, cell] = mixing_in[...]
    for copy in copies[3:]:
        copy.wait()


def visit(refs, stage, step, fill=False):
    if stage is None:
        for i, ref in enumerate(refs):
            step(i, ref)
        return
    if not fill:
        for i, ref in enumerate(refs):
            stage[i] = ref[...]

    def body(i, carry):
        step(i, stage.at[i])
        return carry

    lax.fori_loop(0, len(refs), body, 0)
    if fill:
        for i, ref in enumerate(refs):
            ref[...] = stage[i]


def unpack(tags, refs, stage, core, take):
    if stage is None:
        for (at, swapped), ref in zip(tags, refs):
            take(at, core ^ swapped, ref)
        return
    half = len(refs) // 2
    for swapped in range(2):
        visit(
            refs[swapped * half : (swapped + 1) * half],
            stage,
            lambda i, ref, side=core ^ swapped: take(half - 1 - i, side, ref),
        )


def partner(rounds, at, side):
    return 2 * at + (side ^ (at == rounds - 1) ^ (at == 1))


def arrivals(rounds):
    if rounds == 4:
        return [[(3, 0), (1, 0)], [(2, 0), (0, 0), (3, 1), (1, 1)], [(2, 1), (0, 1)]]
    return [[(at, swapped) for swapped in range(2) for at in reversed(range(rounds))]]


def pack(rounds, own_f, own_g, other_f, other_g, *refs):
    outs, (fields, cots, *stage) = refs[:rounds], refs[rounds:]
    chip, core = place()
    near, rad, feat = own_f.shape
    step = rad + 2 * ROWS
    wide = fields.reshape(2 * near, step, feat)
    edge = jnp.zeros((2 * near, ROWS, feat), F32)
    wide[:, 0:ROWS, :] = edge
    wide[:, ROWS + rad : step, :] = edge
    for side, f, g in ((core, own_f, own_g), (1 - core, other_f, other_g)):
        wide[pl.ds(side * near, near), ROWS : ROWS + rad, :] = f[...].astype(F32)
        cots[pl.ds(side * near, near)] = g[...].astype(F32)
    body = 2 * near * ROWS

    def fill(i, out):
        to = chip ^ partner(rounds, i, core)
        first = pl.multiple_of(to * ROWS, ROWS)
        center = wide[:, pl.ds(pl.multiple_of(first + ROWS, ROWS), ROWS), :]
        out[0:body, :] = center.reshape(body, feat).astype(BF16)
        for h in range(2 * HALO):
            row = first + ROWS + (h - HALO if h < HALO else ROWS + h - HALO)
            at = body + h * 2 * near
            out[at : at + 2 * near, :] = fields[pl.ds(row, 2 * near, stride=step), :].astype(BF16)
        at = body + 2 * HALO * 2 * near
        out[at : at + body, :] = cots[:, pl.ds(first, ROWS), :].reshape(body, feat).astype(BF16)

    visit(outs, stage[0] if stage else None, fill, fill=True)


def receive(tags, rounds, taps, rtaps, filters, mix, blocks, state, stage):
    fields, radial, grads, cots = state
    chip, core = place()
    azim, feat = radial.shape[0] // 2, mix.shape[0]
    step = 2 * ROWS
    wide = fields.reshape(azim, step, feat)
    near = azim // (2 * rounds)
    body = near * ROWS
    weight = [jnp.broadcast_to(filters[taps + j : taps + j + 1, :], (ROWS, feat)) for j in range(rtaps)]

    def take(at, side, block):
        first = (chip ^ partner(rounds, at, side)) * near
        wide[pl.ds(first, near), HALO : HALO + ROWS, :] = (
            block[0:body, :].astype(F32).reshape(near, ROWS, feat)
        )
        for h in range(2 * HALO):
            row = h if h < HALO else ROWS + h
            start = body + h * near
            fields[pl.ds(first * step + row, near, stride=step), :] = block[
                start : start + near, :
            ].astype(F32)
        start = body + 2 * HALO * near
        cot = block[start : start + body, :]
        cots[pl.ds(pl.multiple_of(first * ROWS, body), body), :] = cot
        back = lax.dot_general(cot, mix[...], (((1,), (1,)), ((), ())), preferred_element_type=F32)
        back = back.astype(BF16).astype(F32).reshape(near, ROWS, feat)
        grads[pl.ds(first, near)] = back
        grads[pl.ds(azim + first, near)] = back
        total = weight[0] * wide[pl.ds(first, near), 0:ROWS, :]
        for j in range(1, rtaps):
            total = total + weight[j] * wide[pl.ds(first, near), j : j + ROWS, :]
        radial[pl.ds(first, near)] = total
        radial[pl.ds(azim + first, near)] = total

    unpack(tags, blocks, stage[0] if stage else None, core, take)


def receive_some(tags, rounds, taps, rtaps, old, filters, mix, *refs):
    receive(tags, rounds, taps, rtaps, filters, mix, refs[: len(tags)], refs[len(tags) + old :], ())


def convolve(tags, rounds, taps, rtaps, channels, old, offsets, filters, mix, *refs):
    blocks, state = refs[: len(tags)], refs[len(tags) : len(tags) + old]
    outs, rest = refs[len(tags) + old :][:rounds], refs[len(tags) + old + rounds :]
    if not old:
        state, rest = rest[:4], rest[4:]
    hidden, spread, *stage = rest
    fields, radial, grads, cots = state
    receive(tags, rounds, taps, rtaps, filters, mix, blocks, state, stage)
    chip, core = place()
    azim, feat = radial.shape[0] // 2, mix.shape[0]
    wide = fields.reshape(azim, 2 * ROWS, feat)
    body = azim // (2 * rounds) * ROWS
    weight = [jnp.broadcast_to(filters[k : k + 1, :], (ROWS, feat)) for k in range(taps)]
    ahead = [lax.rem(offsets[k] + azim, azim) for k in range(taps)]
    behind = [lax.rem(azim - offsets[k], azim) for k in range(taps)]

    def slab(n, sums):
        sums = list(sums)
        a = n * SLAB
        grad = grads[pl.ds(a, SLAB)]
        value = jnp.zeros((SLAB, ROWS, feat), F32)
        back = jnp.zeros((SLAB, ROWS, feat), F32)
        for k in range(taps):
            x = radial[pl.ds(a + ahead[k], SLAB)]
            value = value + weight[k] * x
            sums[k] = sums[k] + jnp.sum(x * grad, axis=0)
            back = back + weight[k] * grads[pl.ds(a + behind[k], SLAB)]
        rows = pl.ds(pl.multiple_of(a * ROWS, SLAB * ROWS), SLAB * ROWS)
        hidden[rows, :] = value.reshape(SLAB * ROWS, feat).astype(BF16)
        spread[rows, :] = back.reshape(SLAB * ROWS, feat).astype(BF16)
        for j in range(rtaps):
            sums[taps + j] = sums[taps + j] + jnp.sum(
                wide[pl.ds(a, SLAB), j : j + ROWS, :] * back, axis=0
            )
        return tuple(sums)

    zero = jnp.zeros((ROWS, feat), F32)
    sums = lax.fori_loop(0, azim // SLAB, slab, (zero,) * (taps + rtaps), unroll=2)
    product = lax.dot_general(
        hidden[...], cots[...], (((0,), (0,)), ((), ())), preferred_element_type=F32
    )
    lane = lax.broadcasted_iota(jnp.int32, (channels, feat), 1)
    mixed = jnp.where(lane < channels, product[0:channels], product[channels:feat])
    part = jnp.concatenate([jnp.sum(s, axis=0, keepdims=True) for s in sums] + [mixed], axis=0)
    part = part + pltpu.roll(part, channels, 1)
    few, half = (taps + rtaps) // 2, channels // 2
    low = jnp.concatenate([part[0:few], part[2 * few : 2 * few + half]], axis=0)
    high = jnp.concatenate([part[few : 2 * few], part[2 * few + half : 2 * few + channels]], axis=0)
    lane = lax.broadcasted_iota(jnp.int32, low.shape, 1)
    part = jnp.where(lane < channels, low, high)
    part = jnp.concatenate([part, jnp.zeros((8, feat), F32)], axis=0).astype(BF16)
    for i, out in enumerate(outs):
        to = chip ^ partner(rounds, i, core)
        rows = pl.ds(pl.multiple_of(to * body, body), body)
        out[0:body, :] = hidden[rows, :]
        out[body : 2 * body, :] = spread[rows, :]
        out[2 * body : 2 * body + part.shape[0], :] = part


def collect(tags, rounds, blocks, state, stage):
    hidden, spread, summed = state
    chip, core = place()
    near, feat = hidden.shape[0], hidden.shape[2]
    body = near * ROWS
    mine = pl.multiple_of(core * body, body)

    def take(at, side, block):
        first = pl.multiple_of((chip ^ partner(rounds, at, side)) * ROWS, ROWS)
        hidden[:, pl.ds(first, ROWS), :] = (
            block[pl.ds(mine, body), :].astype(F32).reshape(near, ROWS, feat)
        )
        spread[:, pl.ds(pl.multiple_of(first + ROWS, ROWS), ROWS), :] = (
            block[pl.ds(2 * body + mine, body), :].astype(F32).reshape(near, ROWS, feat)
        )
        summed[...] += block[4 * body : 4 * body + summed.shape[0], :].astype(F32)

    unpack(tags, blocks, stage[0] if stage else None, core, take)


def clear(state):
    hidden, spread, summed = state
    near, rad, feat = hidden.shape
    spread[:, 0:ROWS, :] = jnp.zeros((near, ROWS, feat), F32)
    spread[:, ROWS + rad :, :] = jnp.zeros((near, ROWS, feat), F32)
    summed[...] = jnp.zeros(summed.shape, F32)


def collect_some(tags, rounds, old, *refs):
    state = refs[len(tags) + old :]
    if not old:
        clear(state)
    collect(tags, rounds, refs[: len(tags)], state, ())


def finish(tags, rounds, taps, rtaps, scale, old, field, cot, filters, mix, *refs):
    blocks, state = refs[: len(tags)], refs[len(tags) : len(tags) + old]
    targets, rest = refs[len(tags) + old :][:5], refs[len(tags) + old + 5 :]
    if not old:
        state, rest = rest[:3], rest[3:]
        clear(state)
    hidden, spread, summed = state
    out, grad, azimuth_out, radial_out, mixing_out, sems, *stage = rest
    collect(tags, rounds, blocks, state, stage)
    near, rad, feat = field.shape
    channels = azimuth_out.shape[1]
    sources = (out, grad, azimuth_out, radial_out, mixing_out)
    copies = [pltpu.make_async_copy(*pair, sems.at[i]) for i, pair in enumerate(zip(sources, targets))]
    few, half = (taps + rtaps) // 2, channels // 2
    part = summed[0 : few + half, :] * scale
    azimuth_out[0:few, :] = part[0:few, 0:channels]
    azimuth_out[few:taps, :] = part[0 : taps - few, channels:feat]
    radial_out[...] = part[taps - few : few, channels:feat]
    mixing_out[0:half, :] = part[few : few + half, 0:channels]
    mixing_out[half:channels, :] = part[few : few + half, channels:feat]
    for copy in copies[2:]:
        copy.start()
    flat = hidden[...].reshape(near * rad, feat).astype(BF16)
    mixed = jnp.dot(flat, mix[...], preferred_element_type=F32).reshape(near, rad, feat)
    out[...] = (field[...].astype(F32) + mixed).astype(BF16)
    copies[0].start()
    total = jnp.zeros((near, rad, feat), F32)
    for j in range(rtaps):
        weight = jnp.broadcast_to(filters[taps + j : taps + j + 1, :], (rad, feat))
        first = ROWS + HALO - j
        total = total + weight * spread[:, first : first + rad, :]
    branch = total.astype(BF16).astype(F32)
    grad[...] = (cot[...].astype(F32) + branch).astype(BF16)
    copies[1].start()
    for copy in copies:
        copy.wait()


def call(kernel, ins, outs, scratch, old=0, name=None):
    ins = [
        pltpu.with_memory_space_constraint(x, pltpu.VMEM if x.ndim > 1 else pltpu.SMEM) for x in ins
    ]
    return pl.pallas_call(
        kernel,
        in_specs=[VMEM if x.ndim > 1 else SMEM for x in ins],
        out_specs=[VMEM] * len(outs),
        out_shape=[pltpu.VMEM(*out) for out in outs],
        scratch_shapes=[pltpu.VMEM(*out) for out in scratch],
        input_output_aliases={len(ins) - old + i: i for i in range(old)},
        compiler_params=PARAMS,
        name=name,
    )(*ins)


def swap(x):
    size = lax.axis_size("az")
    return lax.ppermute(x, "az", [(i, i ^ 1) for i in range(size)])


def exchange(messages, unpacked, empty):
    rounds, chips = len(messages), lax.axis_size("az") // 2
    blocks = {}
    for at in reversed(range(rounds)):
        pairs = [(2 * c + k, 2 * (c ^ partner(rounds, at, k)) + k) for c in range(chips) for k in range(2)]
        blocks[at, 0] = lax.ppermute(messages[at], "az", pairs)
    groups, state = arrivals(rounds), []
    for group in groups:
        fresh = [tag for tag in group if not tag[1]]
        if state:
            tied = lax.optimization_barrier(([blocks[tag] for tag in fresh], state))
            state = list(tied[1])
            blocks.update(zip(fresh, tied[0]))
        for at, _ in fresh:
            blocks[at, 1] = swap(blocks[at, 0])
        if group is not groups[-1]:
            state = list(unpacked(group, [blocks[tag] for tag in group], state, empty))
    return groups[-1], [blocks[tag] for tag in groups[-1]], state


def local(fields, cotangent, azimuth_filter, radial_filter, mixing, tap_offsets):
    size = lax.axis_size("az")
    rounds = size // 4
    near, rad, feat = fields.shape
    azim = near * size
    taps, rtaps, channels = tap_offsets.shape[0], radial_filter.shape[0], mixing.shape[0]
    many = rounds > 8
    other_f, other_g = swap(fields), swap(cotangent)
    arguments = (fields, cotangent, azimuth_filter, radial_filter, mixing, tap_offsets)
    kept = [
        pltpu.VMEM(fields.shape, BF16),
        pltpu.VMEM(fields.shape, BF16),
        pltpu.VMEM((taps + rtaps, feat), F32),
        pltpu.VMEM((feat, feat), BF16),
        pltpu.SMEM((taps,), jnp.int32),
    ]
    fields, cotangent, filters, mix, tap_offsets = pl.pallas_call(
        gather,
        in_specs=[pl.BlockSpec(memory_space=pltpu.HBM)] * len(arguments),
        out_specs=[VMEM] * 4 + [SMEM],
        out_shape=kept,
        scratch_shapes=[
            pltpu.VMEM(azimuth_filter.shape, F32),
            pltpu.VMEM(radial_filter.shape, F32),
            pltpu.VMEM(mixing.shape, BF16),
            pltpu.SemaphoreType.DMA((len(arguments),)),
        ],
        compiler_params=PARAMS,
        name="gather",
    )(*(pltpu.with_memory_space_constraint(x, pltpu.HBM) for x in arguments))
    other_f, other_g, fields, cotangent = lax.optimization_barrier(
        (other_f, other_g, fields, cotangent)
    )
    body = 2 * near * ROWS
    length = 2 * body + 2 * HALO * 2 * near
    messages = call(
        functools.partial(pack, rounds),
        (fields, cotangent, other_f, other_g),
        [((length, feat), BF16)] * rounds,
        [((2 * near * (rad + 2 * ROWS), feat), F32), ((2 * near, rad, feat), F32)]
        + [((rounds, length, feat), BF16)] * many,
        name="pack",
    )

    def receiver(tags, blocks, state, empty):
        return call(
            functools.partial(receive_some, tags, rounds, taps, rtaps, len(state)),
            (filters, mix, *blocks, *state),
            empty,
            [],
            old=len(state),
            name="receive",
        )

    flat = ((azim * ROWS, feat), BF16)
    twice = ((2 * azim, ROWS, feat), F32)
    empty = [((azim * 2 * ROWS, feat), F32), twice, twice, flat]
    tags, blocks, state = exchange(messages, receiver, empty)
    sums = (taps + rtaps + channels) // 2 + 8
    messages = call(
        functools.partial(convolve, tags, rounds, taps, rtaps, channels, len(state)),
        (tap_offsets, filters, mix, *blocks, *state),
        [((2 * body + sums, feat), BF16)] * rounds,
        ([] if state else empty)
        + [flat, flat]
        + [((rounds, length, feat), BF16)] * many,
        name="convolve",
    )

    def collector(tags, blocks, state, empty):
        return call(
            functools.partial(collect_some, tags, rounds, len(state)),
            (*blocks, *state),
            empty,
            [],
            old=len(state),
            name="collect",
        )

    empty = [((near, rad, feat), F32), ((near, rad + 2 * ROWS, feat), F32), ((sums, feat), F32)]
    tags, blocks, state = exchange(messages, collector, empty)
    scale = 1.0 / math.sqrt(azim * rad * (feat // channels))
    ins = (fields, cotangent, filters, mix, *blocks, *state)
    outs = [
        (fields.shape, BF16),
        (fields.shape, BF16),
        ((taps, channels), F32),
        ((rtaps, channels), F32),
        ((channels, channels), F32),
    ]
    return pl.pallas_call(
        functools.partial(finish, tags, rounds, taps, rtaps, scale, len(state)),
        in_specs=[VMEM] * len(ins),
        out_specs=[pl.BlockSpec(memory_space=pltpu.HBM)] * len(outs),
        out_shape=[jax.ShapeDtypeStruct(*out) for out in outs],
        scratch_shapes=[pltpu.VMEM(*out) for out in ([] if state else empty) + outs]
        + [pltpu.SemaphoreType.DMA((len(outs),))]
        + [pltpu.VMEM((rounds, 2 * body + sums, feat), BF16)] * many,
        compiler_params=PARAMS,
        name="finish",
    )(*(pltpu.with_memory_space_constraint(x, pltpu.VMEM) for x in ins))


def solution(mesh):
    cells = P(("parts", "az"), None, None)
    parts = P("parts", None)
    return jax.shard_map(
        lambda *args: tuple(local(*args)),
        mesh=mesh,
        in_specs=(cells, cells, P(), P(), P(), P()),
        out_specs=(cells, cells, parts, parts, parts),
        check_vma=False,
    )
```

```python
import functools
import math

import jax
import jax.numpy as jnp
from jax import lax
from jax.experimental import pallas as pl
from jax.experimental.pallas import tpu as pltpu
from jax.sharding import PartitionSpec as P

F32, BF16 = jnp.float32, jnp.bfloat16
VMEM = pl.BlockSpec(memory_space=pltpu.VMEM)
SMEM = pl.BlockSpec(memory_space=pltpu.SMEM)
ROWS = 8
HALO = 3
SLAB = 8
PARAMS = pltpu.CompilerParams(vmem_limit_bytes=56 * 1024 * 1024)


def place():
    at = lax.axis_index("az")
    return at // 2, at % 2


def gather(field, cot, azimuth, radial, mixing, offsets, *refs):
    own_f, own_g, filters, mix, own_offsets, azimuth_in, radial_in, mixing_in, sems = refs
    pairs = (
        (azimuth, azimuth_in),
        (radial, radial_in),
        (mixing, mixing_in),
        (offsets, own_offsets),
        (field, own_f),
        (cot, own_g),
    )
    copies = [pltpu.make_async_copy(*pair, sems.at[i]) for i, pair in enumerate(pairs)]
    for copy in copies:
        copy.start()
    filters[...] = jnp.zeros(filters.shape, F32)
    mix[...] = jnp.zeros(mix.shape, BF16)
    for copy in copies[:3]:
        copy.wait()
    taps, channels = azimuth_in.shape
    rtaps, feat = radial_in.shape[0], mix.shape[0]
    for low in range(0, feat, channels):
        cell = slice(low, low + channels)
        filters[0:taps, cell] = azimuth_in[...]
        filters[taps : taps + rtaps, cell] = radial_in[...]
        mix[cell, cell] = mixing_in[...]
    for copy in copies[3:]:
        copy.wait()


def visit(refs, stage, step, fill=False):
    if stage is None:
        for i, ref in enumerate(refs):
            step(i, ref)
        return
    if not fill:
        for i, ref in enumerate(refs):
            stage[i] = ref[...]

    def body(i, carry):
        step(i, stage.at[i])
        return carry

    lax.fori_loop(0, len(refs), body, 0)
    if fill:
        for i, ref in enumerate(refs):
            ref[...] = stage[i]


def unpack(tags, refs, stage, core, take):
    if stage is None:
        for (at, swapped), ref in zip(tags, refs):
            take(at, core ^ swapped, ref)
        return
    half = len(refs) // 2
    for swapped in range(2):
        visit(
            refs[swapped * half : (swapped + 1) * half],
            stage,
            lambda i, ref, side=core ^ swapped: take(half - 1 - i, side, ref),
        )


def plan(rounds):
    if rounds == 4:
        return ((3, 1, 2, 0), (3,)), ((3, 1, 2, 0), (3, 1))
    descending = tuple(reversed(range(rounds)))
    return (descending, ()), (descending, ())


def partner(route, at, side):
    return 2 * at + (side ^ (at in route[1]) if isinstance(at, int) else side)


def arrivals(route):
    order = route[0]
    if len(order) != 4:
        return [[(at, swapped) for swapped in range(2) for at in order]]
    first, second = order[:2], order[2:]
    return [
        [(at, 0) for at in first],
        [(at, 0) for at in second] + [(at, 1) for at in first],
        [(at, 1) for at in second],
    ]


def pack(route, own_f, own_g, other_f, other_g, *refs):
    rounds = len(route[0])
    outs, (fields, cots, *stage) = refs[:rounds], refs[rounds:]
    chip, core = place()
    near, rad, feat = own_f.shape
    step = rad + 2 * ROWS
    wide = fields.reshape(2 * near, step, feat)
    edge = jnp.zeros((2 * near, ROWS, feat), F32)
    wide[:, 0:ROWS, :] = edge
    wide[:, ROWS + rad : step, :] = edge
    for side, f, g in ((core, own_f, own_g), (1 - core, other_f, other_g)):
        wide[pl.ds(side * near, near), ROWS : ROWS + rad, :] = f[...].astype(F32)
        cots[pl.ds(side * near, near)] = g[...].astype(F32)
    body = 2 * near * ROWS

    half = feat // 2

    def beside(moved, kept, cell):
        lane = lax.broadcasted_iota(jnp.int32, moved.shape, 1)
        return jnp.where((lane < half) == (cell == 1), pltpu.roll(moved, half, 1), kept).astype(BF16)

    def fill(i, out):
        to = chip ^ partner(route, rounds - 1 - i, core)
        cell = to % 2
        first = to // 2 * (2 * ROWS)

        def rows(ref, start, second):
            start = pl.multiple_of(start + ROWS * second, ROWS)
            return ref[:, pl.ds(start, ROWS), :].reshape(body, feat)

        def pair(ref, start):
            return beside(rows(ref, start, 1 - cell), rows(ref, start, cell), cell)

        out[0:body, :] = pair(wide, first + ROWS)
        for h in range(HALO):
            at = body + h * 2 * near
            above, between = first + ROWS - HALO + h, HALO + 2 * ROWS
            out[at : at + 2 * near, :] = beside(
                fields[pl.ds(above + between * (1 - cell), 2 * near, stride=step), :],
                fields[pl.ds(above + between * cell, 2 * near, stride=step), :],
                cell,
            )
        at = body + HALO * 2 * near
        out[at : at + body, :] = pair(cots, first)

    visit(outs, stage[0] if stage else None, fill, fill=True)


def receive(tags, route, taps, rtaps, filters, mix, blocks, state, stage):
    fields, radial, grads, cots = state
    chip, core = place()
    rounds = len(route[0])
    azim, feat = radial.shape[0] // 2, mix.shape[0]
    step = 2 * ROWS
    wide = fields.reshape(azim, step, feat)
    near = azim // (2 * rounds)
    body = near * ROWS
    weight = [jnp.broadcast_to(filters[taps + j : taps + j + 1, :], (ROWS, feat)) for j in range(rtaps)]

    def take(at, side, block):
        first = (chip ^ partner(route, at, side)) * near
        wide[pl.ds(first, near), HALO : HALO + ROWS, :] = (
            block[0:body, :].astype(F32).reshape(near, ROWS, feat)
        )
        lane = lax.broadcasted_iota(jnp.int32, (near, feat), 1)
        for h in range(HALO):
            start = body + h * near
            edge = block[start : start + near, :].astype(F32)

            def row(r):
                return pl.ds(first * step + r, near, stride=step)

            lower = pltpu.roll(fields[row(ROWS + h), :], feat // 2, 1)
            upper = pltpu.roll(fields[row(HALO + h), :], feat // 2, 1)
            fields[row(h), :] = jnp.where(lane < feat // 2, edge, lower)
            fields[row(HALO + ROWS + h), :] = jnp.where(lane < feat // 2, upper, edge)
        start = body + HALO * near
        cot = block[start : start + body, :]
        cots[pl.ds(pl.multiple_of(first * ROWS, body), body), :] = cot
        back = lax.dot_general(cot, mix[...], (((1,), (1,)), ((), ())), preferred_element_type=F32)
        back = back.astype(BF16).astype(F32).reshape(near, ROWS, feat)
        grads[pl.ds(first, near)] = back
        grads[pl.ds(azim + first, near)] = back
        total = weight[0] * wide[pl.ds(first, near), 0:ROWS, :]
        for j in range(1, rtaps):
            total = total + weight[j] * wide[pl.ds(first, near), j : j + ROWS, :]
        radial[pl.ds(first, near)] = total
        radial[pl.ds(azim + first, near)] = total

    unpack(tags, blocks, stage[0] if stage else None, core, take)


def receive_some(tags, route, taps, rtaps, old, filters, mix, *refs):
    receive(tags, route, taps, rtaps, filters, mix, refs[: len(tags)], refs[len(tags) + old :], ())


def convolve(tags, route_in, route, taps, rtaps, channels, old, offsets, filters, mix, *refs):
    rounds = len(route[0])
    blocks, state = refs[: len(tags)], refs[len(tags) : len(tags) + old]
    outs, rest = refs[len(tags) + old :][:rounds], refs[len(tags) + old + rounds :]
    if not old:
        state, rest = rest[:4], rest[4:]
    hidden, spread, *stage = rest
    fields, radial, grads, cots = state
    receive(tags, route_in, taps, rtaps, filters, mix, blocks, state, stage)
    chip, core = place()
    azim, feat = radial.shape[0] // 2, mix.shape[0]
    wide = fields.reshape(azim, 2 * ROWS, feat)
    body = azim // (2 * rounds) * ROWS
    weight = [jnp.broadcast_to(filters[k : k + 1, :], (ROWS, feat)) for k in range(taps)]
    ahead = [lax.rem(offsets[k] + azim, azim) for k in range(taps)]
    behind = [lax.rem(azim - offsets[k], azim) for k in range(taps)]

    def slab(n, sums):
        sums = list(sums)
        a = n * SLAB
        grad = grads[pl.ds(a, SLAB)]
        value = jnp.zeros((SLAB, ROWS, feat), F32)
        back = jnp.zeros((SLAB, ROWS, feat), F32)
        for k in range(taps):
            x = radial[pl.ds(a + ahead[k], SLAB)]
            value = value + weight[k] * x
            sums[k] = sums[k] + jnp.sum(x * grad, axis=0)
            back = back + weight[k] * grads[pl.ds(a + behind[k], SLAB)]
        rows = pl.ds(pl.multiple_of(a * ROWS, SLAB * ROWS), SLAB * ROWS)
        hidden[rows, :] = value.reshape(SLAB * ROWS, feat).astype(BF16)
        spread[rows, :] = back.reshape(SLAB * ROWS, feat).astype(BF16)
        for j in range(rtaps):
            sums[taps + j] = sums[taps + j] + jnp.sum(
                wide[pl.ds(a, SLAB), j : j + ROWS, :] * back, axis=0
            )
        return tuple(sums)

    zero = jnp.zeros((ROWS, feat), F32)
    sums = lax.fori_loop(0, azim // SLAB, slab, (zero,) * (taps + rtaps), unroll=2)
    product = lax.dot_general(
        hidden[...], cots[...], (((0,), (0,)), ((), ())), preferred_element_type=F32
    )
    lane = lax.broadcasted_iota(jnp.int32, (channels, feat), 1)
    mixed = jnp.where(lane < channels, product[0:channels], product[channels:feat])
    part = jnp.concatenate([jnp.sum(s, axis=0, keepdims=True) for s in sums] + [mixed], axis=0)
    part = part + pltpu.roll(part, channels, 1)
    few, half = (taps + rtaps) // 2, channels // 2
    low = jnp.concatenate([part[0:few], part[2 * few : 2 * few + half]], axis=0)
    high = jnp.concatenate([part[few : 2 * few], part[2 * few + half : 2 * few + channels]], axis=0)
    lane = lax.broadcasted_iota(jnp.int32, low.shape, 1)
    part = jnp.where(lane < channels, low, high)
    part = jnp.concatenate([part, jnp.zeros((8, feat), F32)], axis=0).astype(BF16)
    for i, out in enumerate(outs):
        to = chip ^ partner(route, rounds - 1 - i, core)
        rows = pl.ds(pl.multiple_of(to * body, body), body)
        out[0:body, :] = hidden[rows, :]
        out[body : 2 * body, :] = spread[rows, :]
        out[2 * body : 2 * body + part.shape[0], :] = part


def collect(tags, route, blocks, state, stage):
    hidden, spread, summed = state
    chip, core = place()
    near, feat = hidden.shape[0], hidden.shape[2]
    body = near * ROWS
    mine = pl.multiple_of(core * body, body)

    half = feat // 2
    lane = lax.broadcasted_iota(jnp.int32, (body, feat), 1)

    def put(ref, start, value, cell):
        start = pl.multiple_of(start, ROWS)
        old = ref[:, pl.ds(start, ROWS), :].reshape(body, feat)
        new = jnp.where((lane >= half) == (cell == 1), value, old)
        ref[:, pl.ds(start, ROWS), :] = new.reshape(near, ROWS, feat)

    def take(at, side, block):
        source = chip ^ partner(route, at, side)
        first, cell = source // 2 * (2 * ROWS), source % 2
        for ref, start, edge in ((hidden, mine, 0), (spread, 2 * body + mine, ROWS)):
            value = block[pl.ds(start, body), :].astype(F32)
            put(ref, first + edge + ROWS * cell, value, cell)
            put(ref, first + edge + ROWS * (1 - cell), pltpu.roll(value, half, 1), cell)
        summed[...] += block[4 * body : 4 * body + summed.shape[0], :].astype(F32)

    unpack(tags, blocks, stage[0] if stage else None, core, take)


def clear(state):
    hidden, spread, summed = state
    near, rad, feat = hidden.shape
    spread[:, 0:ROWS, :] = jnp.zeros((near, ROWS, feat), F32)
    spread[:, ROWS + rad :, :] = jnp.zeros((near, ROWS, feat), F32)
    summed[...] = jnp.zeros(summed.shape, F32)


def collect_some(tags, route, old, *refs):
    state = refs[len(tags) + old :]
    if not old:
        clear(state)
    collect(tags, route, refs[: len(tags)], state, ())


def finish(tags, route, taps, rtaps, scale, old, field, cot, filters, mix, *refs):
    blocks, state = refs[: len(tags)], refs[len(tags) : len(tags) + old]
    targets, rest = refs[len(tags) + old :][:5], refs[len(tags) + old + 5 :]
    if not old:
        state, rest = rest[:3], rest[3:]
        clear(state)
    hidden, spread, summed = state
    out, grad, azimuth_out, radial_out, mixing_out, sems, *stage = rest
    collect(tags, route, blocks, state, stage)
    near, rad, feat = field.shape
    channels = azimuth_out.shape[1]
    sources = (out, grad, azimuth_out, radial_out, mixing_out)
    copies = [pltpu.make_async_copy(*pair, sems.at[i]) for i, pair in enumerate(zip(sources, targets))]
    few, half = (taps + rtaps) // 2, channels // 2
    part = summed[0 : few + half, :] * scale
    azimuth_out[0:few, :] = part[0:few, 0:channels]
    azimuth_out[few:taps, :] = part[0 : taps - few, channels:feat]
    radial_out[...] = part[taps - few : few, channels:feat]
    mixing_out[0:half, :] = part[few : few + half, 0:channels]
    mixing_out[half:channels, :] = part[few : few + half, channels:feat]
    for copy in copies[2:]:
        copy.start()
    flat = hidden[...].reshape(near * rad, feat).astype(BF16)
    mixed = jnp.dot(flat, mix[...], preferred_element_type=F32).reshape(near, rad, feat)
    out[...] = (field[...].astype(F32) + mixed).astype(BF16)
    copies[0].start()
    total = jnp.zeros((near, rad, feat), F32)
    for j in range(rtaps):
        weight = jnp.broadcast_to(filters[taps + j : taps + j + 1, :], (rad, feat))
        first = ROWS + HALO - j
        total = total + weight * spread[:, first : first + rad, :]
    branch = total.astype(BF16).astype(F32)
    grad[...] = (cot[...].astype(F32) + branch).astype(BF16)
    copies[1].start()
    for copy in copies:
        copy.wait()


def call(kernel, ins, outs, scratch, old=0, name=None):
    ins = [
        pltpu.with_memory_space_constraint(x, pltpu.VMEM if x.ndim > 1 else pltpu.SMEM) for x in ins
    ]
    return pl.pallas_call(
        kernel,
        in_specs=[VMEM if x.ndim > 1 else SMEM for x in ins],
        out_specs=[VMEM] * len(outs),
        out_shape=[pltpu.VMEM(*out) for out in outs],
        scratch_shapes=[pltpu.VMEM(*out) for out in scratch],
        input_output_aliases={len(ins) - old + i: i for i in range(old)},
        compiler_params=PARAMS,
        name=name,
    )(*ins)


def swap(x):
    size = lax.axis_size("az")
    return lax.ppermute(x, "az", [(i, i ^ 1) for i in range(size)])


def exchange(messages, route, unpacked, empty):
    rounds, chips = len(messages), lax.axis_size("az") // 2
    blocks = {}
    for at in route[0]:
        pairs = [(2 * c + k, 2 * (c ^ partner(route, at, k)) + k) for c in range(chips) for k in range(2)]
        blocks[at, 0] = lax.ppermute(messages[rounds - 1 - at], "az", pairs)
    groups, state = arrivals(route), []
    for group in groups:
        fresh = [tag for tag in group if not tag[1]]
        if state:
            tied = lax.optimization_barrier(([blocks[tag] for tag in fresh], state))
            state = list(tied[1])
            blocks.update(zip(fresh, tied[0]))
        for at, _ in fresh:
            blocks[at, 1] = swap(blocks[at, 0])
        if group is not groups[-1]:
            state = list(unpacked(group, [blocks[tag] for tag in group], state, empty))
    return groups[-1], [blocks[tag] for tag in groups[-1]], state


def local(fields, cotangent, azimuth_filter, radial_filter, mixing, tap_offsets):
    size = lax.axis_size("az")
    rounds = size // 4
    near, rad, feat = fields.shape
    azim = near * size
    taps, rtaps, channels = tap_offsets.shape[0], radial_filter.shape[0], mixing.shape[0]
    many = rounds > 8
    first, second = plan(rounds)
    other_f, other_g = swap(fields), swap(cotangent)
    arguments = (fields, cotangent, azimuth_filter, radial_filter, mixing, tap_offsets)
    kept = [
        pltpu.VMEM(fields.shape, BF16),
        pltpu.VMEM(fields.shape, BF16),
        pltpu.VMEM((taps + rtaps, feat), F32),
        pltpu.VMEM((feat, feat), BF16),
        pltpu.SMEM((taps,), jnp.int32),
    ]
    fields, cotangent, filters, mix, tap_offsets = pl.pallas_call(
        gather,
        in_specs=[pl.BlockSpec(memory_space=pltpu.HBM)] * len(arguments),
        out_specs=[VMEM] * 4 + [SMEM],
        out_shape=kept,
        scratch_shapes=[
            pltpu.VMEM(azimuth_filter.shape, F32),
            pltpu.VMEM(radial_filter.shape, F32),
            pltpu.VMEM(mixing.shape, BF16),
            pltpu.SemaphoreType.DMA((len(arguments),)),
        ],
        compiler_params=PARAMS,
        name="gather",
    )(*(pltpu.with_memory_space_constraint(x, pltpu.HBM) for x in arguments))
    other_f, other_g, fields, cotangent = lax.optimization_barrier(
        (other_f, other_g, fields, cotangent)
    )
    body = 2 * near * ROWS
    length = 2 * body + HALO * 2 * near
    messages = call(
        functools.partial(pack, first),
        (fields, cotangent, other_f, other_g),
        [((length, feat), BF16)] * rounds,
        [((2 * near * (rad + 2 * ROWS), feat), F32), ((2 * near, rad, feat), F32)]
        + [((rounds, length, feat), BF16)] * many,
        name="pack",
    )

    def receiver(tags, blocks, state, empty):
        return call(
            functools.partial(receive_some, tags, first, taps, rtaps, len(state)),
            (filters, mix, *blocks, *state),
            empty,
            [],
            old=len(state),
            name="receive",
        )

    flat = ((azim * ROWS, feat), BF16)
    twice = ((2 * azim, ROWS, feat), F32)
    empty = [((azim * 2 * ROWS, feat), F32), twice, twice, flat]
    tags, blocks, state = exchange(messages, first, receiver, empty)
    sums = (taps + rtaps + channels) // 2 + 8
    messages = call(
        functools.partial(convolve, tags, first, second, taps, rtaps, channels, len(state)),
        (tap_offsets, filters, mix, *blocks, *state),
        [((2 * body + sums, feat), BF16)] * rounds,
        ([] if state else empty)
        + [flat, flat]
        + [((rounds, length, feat), BF16)] * many,
        name="convolve",
    )

    def collector(tags, blocks, state, empty):
        return call(
            functools.partial(collect_some, tags, second, len(state)),
            (*blocks, *state),
            empty,
            [],
            old=len(state),
            name="collect",
        )

    empty = [((near, rad, feat), F32), ((near, rad + 2 * ROWS, feat), F32), ((sums, feat), F32)]
    tags, blocks, state = exchange(messages, second, collector, empty)
    scale = 1.0 / math.sqrt(azim * rad * (feat // channels))
    ins = (fields, cotangent, filters, mix, *blocks, *state)
    outs = [
        (fields.shape, BF16),
        (fields.shape, BF16),
        ((taps, channels), F32),
        ((rtaps, channels), F32),
        ((channels, channels), F32),
    ]
    return pl.pallas_call(
        functools.partial(finish, tags, second, taps, rtaps, scale, len(state)),
        in_specs=[VMEM] * len(ins),
        out_specs=[pl.BlockSpec(memory_space=pltpu.HBM)] * len(outs),
        out_shape=[jax.ShapeDtypeStruct(*out) for out in outs],
        scratch_shapes=[pltpu.VMEM(*out) for out in ([] if state else empty) + outs]
        + [pltpu.SemaphoreType.DMA((len(outs),))]
        + [pltpu.VMEM((rounds, 2 * body + sums, feat), BF16)] * many,
        compiler_params=PARAMS,
        name="finish",
    )(*(pltpu.with_memory_space_constraint(x, pltpu.VMEM) for x in ins))


def solution(mesh):
    cells = P(("parts", "az"), None, None)
    parts = P("parts", None)
    return jax.shard_map(
        lambda *args: tuple(local(*args)),
        mesh=mesh,
        in_specs=(cells, cells, P(), P(), P(), P()),
        out_specs=(cells, cells, parts, parts, parts),
        check_vma=False,
    )
```

```python
import functools
import math

import jax
import jax.numpy as jnp
from jax import lax
from jax.experimental import pallas as pl
from jax.experimental.pallas import tpu as pltpu
from jax.sharding import PartitionSpec as P

F32, BF16 = jnp.float32, jnp.bfloat16
VMEM = pl.BlockSpec(memory_space=pltpu.VMEM)
SMEM = pl.BlockSpec(memory_space=pltpu.SMEM)
ROWS = 8
HALO = 3
SLAB = 8
PARAMS = pltpu.CompilerParams(vmem_limit_bytes=56 * 1024 * 1024)


def place():
    at = lax.axis_index("az")
    return at // 2, at % 2


def gather(field, cot, azimuth, radial, mixing, offsets, *refs):
    own_f, own_g, filters, mix, own_offsets, azimuth_in, radial_in, mixing_in, sems = refs
    pairs = (
        (azimuth, azimuth_in),
        (radial, radial_in),
        (mixing, mixing_in),
        (offsets, own_offsets),
        (field, own_f),
        (cot, own_g),
    )
    copies = [pltpu.make_async_copy(*pair, sems.at[i]) for i, pair in enumerate(pairs)]
    for copy in copies:
        copy.start()
    filters[...] = jnp.zeros(filters.shape, F32)
    mix[...] = jnp.zeros(mix.shape, BF16)
    for copy in copies[:3]:
        copy.wait()
    taps, channels = azimuth_in.shape
    rtaps, feat = radial_in.shape[0], mix.shape[0]
    for low in range(0, feat, channels):
        cell = slice(low, low + channels)
        filters[0:taps, cell] = azimuth_in[...]
        filters[taps : taps + rtaps, cell] = radial_in[...]
        mix[cell, cell] = mixing_in[...]
    for copy in copies[3:]:
        copy.wait()


def visit(refs, stage, step, fill=False):
    if stage is None:
        for i, ref in enumerate(refs):
            step(i, ref)
        return
    if not fill:
        for i, ref in enumerate(refs):
            stage[i] = ref[...]

    def body(i, carry):
        step(i, stage.at[i])
        return carry

    lax.fori_loop(0, len(refs), body, 0)
    if fill:
        for i, ref in enumerate(refs):
            ref[...] = stage[i]


def unpack(tags, refs, stage, core, take):
    if stage is None:
        for (at, swapped), ref in zip(tags, refs):
            take(at, core ^ swapped, ref)
        return
    half = len(refs) // 2
    for swapped in range(2):
        visit(
            refs[swapped * half : (swapped + 1) * half],
            stage,
            lambda i, ref, side=core ^ swapped: take(half - 1 - i, side, ref),
        )


def plan(rounds):
    if rounds == 4:
        return ((3, 1, 2, 0), (3,), 3), ((3, 1, 2, 0), (3, 1), 2)
    descending = tuple(reversed(range(rounds)))
    return (descending, (), 1), (descending, (), 1)


def partner(route, at, side):
    return 2 * at + (side ^ (at in route[1]) if isinstance(at, int) else side)


def arrivals(route):
    order = route[0]
    if len(order) != 4:
        return [[(at, swapped) for swapped in range(2) for at in order]]
    a, b, c, d = order
    if route[2] == 2:
        return [[(a, 0), (b, 0), (a, 1), (c, 0), (d, 0)], [(b, 1), (c, 1), (d, 1)]]
    return [[(a, 0), (b, 0)], [(c, 0), (d, 0), (a, 1), (b, 1)], [(c, 1), (d, 1)]]


def pack(route, own_f, own_g, other_f, other_g, *refs):
    rounds = len(route[0])
    outs, (fields, cots, *stage) = refs[:rounds], refs[rounds:]
    chip, core = place()
    near, rad, feat = own_f.shape
    step = rad + 2 * ROWS
    wide = fields.reshape(2 * near, step, feat)
    edge = jnp.zeros((2 * near, ROWS, feat), F32)
    wide[:, 0:ROWS, :] = edge
    wide[:, ROWS + rad : step, :] = edge
    for side, f, g in ((core, own_f, own_g), (1 - core, other_f, other_g)):
        wide[pl.ds(side * near, near), ROWS : ROWS + rad, :] = f[...].astype(F32)
        cots[pl.ds(side * near, near)] = g[...].astype(F32)
    body = 2 * near * ROWS

    half = feat // 2

    def beside(moved, kept, cell):
        lane = lax.broadcasted_iota(jnp.int32, moved.shape, 1)
        return jnp.where((lane < half) == (cell == 1), pltpu.roll(moved, half, 1), kept).astype(BF16)

    def fill(i, out):
        to = chip ^ partner(route, rounds - 1 - i, core)
        cell = to % 2
        first = to // 2 * (2 * ROWS)

        def rows(ref, start, second):
            start = pl.multiple_of(start + ROWS * second, ROWS)
            return ref[:, pl.ds(start, ROWS), :].reshape(body, feat)

        def pair(ref, start):
            return beside(rows(ref, start, 1 - cell), rows(ref, start, cell), cell)

        out[0:body, :] = pair(wide, first + ROWS)
        for h in range(HALO):
            at = body + h * 2 * near
            above, between = first + ROWS - HALO + h, HALO + 2 * ROWS
            out[at : at + 2 * near, :] = beside(
                fields[pl.ds(above + between * (1 - cell), 2 * near, stride=step), :],
                fields[pl.ds(above + between * cell, 2 * near, stride=step), :],
                cell,
            )
        at = body + HALO * 2 * near
        out[at : at + body, :] = pair(cots, first)

    visit(outs, stage[0] if stage else None, fill, fill=True)


def receive(tags, route, taps, rtaps, filters, mix, blocks, state, stage):
    fields, radial, grads, cots = state
    chip, core = place()
    rounds = len(route[0])
    azim, feat = radial.shape[0] // 2, mix.shape[0]
    step = 2 * ROWS
    wide = fields.reshape(azim, step, feat)
    near = azim // (2 * rounds)
    body = near * ROWS
    weight = [jnp.broadcast_to(filters[taps + j : taps + j + 1, :], (ROWS, feat)) for j in range(rtaps)]

    def take(at, side, block):
        first = (chip ^ partner(route, at, side)) * near
        wide[pl.ds(first, near), HALO : HALO + ROWS, :] = (
            block[0:body, :].astype(F32).reshape(near, ROWS, feat)
        )
        lane = lax.broadcasted_iota(jnp.int32, (near, feat), 1)
        for h in range(HALO):
            start = body + h * near
            edge = block[start : start + near, :].astype(F32)

            def row(r):
                return pl.ds(first * step + r, near, stride=step)

            lower = pltpu.roll(fields[row(ROWS + h), :], feat // 2, 1)
            upper = pltpu.roll(fields[row(HALO + h), :], feat // 2, 1)
            fields[row(h), :] = jnp.where(lane < feat // 2, edge, lower)
            fields[row(HALO + ROWS + h), :] = jnp.where(lane < feat // 2, upper, edge)
        start = body + HALO * near
        cot = block[start : start + body, :]
        cots[pl.ds(pl.multiple_of(first * ROWS, body), body), :] = cot
        back = lax.dot_general(cot, mix[...], (((1,), (1,)), ((), ())), preferred_element_type=F32)
        back = back.astype(BF16).astype(F32).reshape(near, ROWS, feat)
        grads[pl.ds(first, near)] = back
        grads[pl.ds(azim + first, near)] = back
        total = weight[0] * wide[pl.ds(first, near), 0:ROWS, :]
        for j in range(1, rtaps):
            total = total + weight[j] * wide[pl.ds(first, near), j : j + ROWS, :]
        radial[pl.ds(first, near)] = total
        radial[pl.ds(azim + first, near)] = total

    unpack(tags, blocks, stage[0] if stage else None, core, take)


def receive_some(tags, route, taps, rtaps, old, filters, mix, *refs):
    receive(tags, route, taps, rtaps, filters, mix, refs[: len(tags)], refs[len(tags) + old :], ())


def convolve(tags, route_in, route, taps, rtaps, channels, old, offsets, filters, mix, *refs):
    rounds = len(route[0])
    blocks, state = refs[: len(tags)], refs[len(tags) : len(tags) + old]
    outs, rest = refs[len(tags) + old :][:rounds], refs[len(tags) + old + rounds :]
    if not old:
        state, rest = rest[:4], rest[4:]
    hidden, spread, *stage = rest
    fields, radial, grads, cots = state
    receive(tags, route_in, taps, rtaps, filters, mix, blocks, state, stage)
    chip, core = place()
    azim, feat = radial.shape[0] // 2, mix.shape[0]
    wide = fields.reshape(azim, 2 * ROWS, feat)
    body = azim // (2 * rounds) * ROWS
    weight = [jnp.broadcast_to(filters[k : k + 1, :], (ROWS, feat)) for k in range(taps)]
    ahead = [lax.rem(offsets[k] + azim, azim) for k in range(taps)]
    behind = [lax.rem(azim - offsets[k], azim) for k in range(taps)]

    def slab(n, sums):
        sums = list(sums)
        a = n * SLAB
        grad = grads[pl.ds(a, SLAB)]
        value = jnp.zeros((SLAB, ROWS, feat), F32)
        back = jnp.zeros((SLAB, ROWS, feat), F32)
        for k in range(taps):
            x = radial[pl.ds(a + ahead[k], SLAB)]
            value = value + weight[k] * x
            sums[k] = sums[k] + jnp.sum(x * grad, axis=0)
            back = back + weight[k] * grads[pl.ds(a + behind[k], SLAB)]
        rows = pl.ds(pl.multiple_of(a * ROWS, SLAB * ROWS), SLAB * ROWS)
        hidden[rows, :] = value.reshape(SLAB * ROWS, feat).astype(BF16)
        spread[rows, :] = back.reshape(SLAB * ROWS, feat).astype(BF16)
        for j in range(rtaps):
            sums[taps + j] = sums[taps + j] + jnp.sum(
                wide[pl.ds(a, SLAB), j : j + ROWS, :] * back, axis=0
            )
        return tuple(sums)

    zero = jnp.zeros((ROWS, feat), F32)
    sums = lax.fori_loop(0, azim // SLAB, slab, (zero,) * (taps + rtaps), unroll=2)
    product = lax.dot_general(
        hidden[...], cots[...], (((0,), (0,)), ((), ())), preferred_element_type=F32
    )
    lane = lax.broadcasted_iota(jnp.int32, (channels, feat), 1)
    mixed = jnp.where(lane < channels, product[0:channels], product[channels:feat])
    part = jnp.concatenate([jnp.sum(s, axis=0, keepdims=True) for s in sums] + [mixed], axis=0)
    part = part + pltpu.roll(part, channels, 1)
    few, half = (taps + rtaps) // 2, channels // 2
    low = jnp.concatenate([part[0:few], part[2 * few : 2 * few + half]], axis=0)
    high = jnp.concatenate([part[few : 2 * few], part[2 * few + half : 2 * few + channels]], axis=0)
    lane = lax.broadcasted_iota(jnp.int32, low.shape, 1)
    part = jnp.where(lane < channels, low, high)
    part = jnp.concatenate([part, jnp.zeros((8, feat), F32)], axis=0).astype(BF16)
    for i, out in enumerate(outs):
        to = chip ^ partner(route, rounds - 1 - i, core)
        rows = pl.ds(pl.multiple_of(to * body, body), body)
        out[0:body, :] = hidden[rows, :]
        out[body : 2 * body, :] = spread[rows, :]
        out[2 * body : 2 * body + part.shape[0], :] = part


def collect(tags, route, blocks, state, stage):
    hidden, spread, summed = state
    chip, core = place()
    near, feat = hidden.shape[0], hidden.shape[2]
    body = near * ROWS
    mine = pl.multiple_of(core * body, body)

    half = feat // 2
    lane = lax.broadcasted_iota(jnp.int32, (body, feat), 1)

    def put(ref, start, value, cell):
        start = pl.multiple_of(start, ROWS)
        old = ref[:, pl.ds(start, ROWS), :].reshape(body, feat)
        new = jnp.where((lane >= half) == (cell == 1), value, old)
        ref[:, pl.ds(start, ROWS), :] = new.reshape(near, ROWS, feat)

    def take(at, side, block):
        source = chip ^ partner(route, at, side)
        first, cell = source // 2 * (2 * ROWS), source % 2
        for ref, start, edge in ((hidden, mine, 0), (spread, 2 * body + mine, ROWS)):
            value = block[pl.ds(start, body), :].astype(F32)
            put(ref, first + edge + ROWS * cell, value, cell)
            put(ref, first + edge + ROWS * (1 - cell), pltpu.roll(value, half, 1), cell)
        summed[...] += block[4 * body : 4 * body + summed.shape[0], :].astype(F32)

    unpack(tags, blocks, stage[0] if stage else None, core, take)


def clear(state):
    hidden, spread, summed = state
    near, rad, feat = hidden.shape
    spread[:, 0:ROWS, :] = jnp.zeros((near, ROWS, feat), F32)
    spread[:, ROWS + rad :, :] = jnp.zeros((near, ROWS, feat), F32)
    summed[...] = jnp.zeros(summed.shape, F32)


def collect_some(tags, route, old, *refs):
    state = refs[len(tags) + old :]
    if not old:
        clear(state)
    collect(tags, route, refs[: len(tags)], state, ())


def finish(tags, route, taps, rtaps, scale, old, field, cot, filters, mix, *refs):
    blocks, state = refs[: len(tags)], refs[len(tags) : len(tags) + old]
    targets, rest = refs[len(tags) + old :][:5], refs[len(tags) + old + 5 :]
    if not old:
        state, rest = rest[:3], rest[3:]
        clear(state)
    hidden, spread, summed = state
    out, grad, azimuth_out, radial_out, mixing_out, sems, *stage = rest
    collect(tags, route, blocks, state, stage)
    near, rad, feat = field.shape
    channels = azimuth_out.shape[1]
    sources = (out, grad, azimuth_out, radial_out, mixing_out)
    copies = [pltpu.make_async_copy(*pair, sems.at[i]) for i, pair in enumerate(zip(sources, targets))]
    few, half = (taps + rtaps) // 2, channels // 2
    part = summed[0 : few + half, :] * scale
    azimuth_out[0:few, :] = part[0:few, 0:channels]
    azimuth_out[few:taps, :] = part[0 : taps - few, channels:feat]
    radial_out[...] = part[taps - few : few, channels:feat]
    mixing_out[0:half, :] = part[few : few + half, 0:channels]
    mixing_out[half:channels, :] = part[few : few + half, channels:feat]
    for copy in copies[2:]:
        copy.start()
    flat = hidden[...].reshape(near * rad, feat).astype(BF16)
    mixed = jnp.dot(flat, mix[...], preferred_element_type=F32).reshape(near, rad, feat)
    out[...] = (field[...].astype(F32) + mixed).astype(BF16)
    copies[0].start()
    total = jnp.zeros((near, rad, feat), F32)
    for j in range(rtaps):
        weight = jnp.broadcast_to(filters[taps + j : taps + j + 1, :], (rad, feat))
        first = ROWS + HALO - j
        total = total + weight * spread[:, first : first + rad, :]
    branch = total.astype(BF16).astype(F32)
    grad[...] = (cot[...].astype(F32) + branch).astype(BF16)
    copies[1].start()
    for copy in copies:
        copy.wait()


def call(kernel, ins, outs, scratch, old=0, name=None):
    ins = [
        pltpu.with_memory_space_constraint(x, pltpu.VMEM if x.ndim > 1 else pltpu.SMEM) for x in ins
    ]
    return pl.pallas_call(
        kernel,
        in_specs=[VMEM if x.ndim > 1 else SMEM for x in ins],
        out_specs=[VMEM] * len(outs),
        out_shape=[pltpu.VMEM(*out) for out in outs],
        scratch_shapes=[pltpu.VMEM(*out) for out in scratch],
        input_output_aliases={len(ins) - old + i: i for i in range(old)},
        compiler_params=PARAMS,
        name=name,
    )(*ins)


def swap(x):
    size = lax.axis_size("az")
    return lax.ppermute(x, "az", [(i, i ^ 1) for i in range(size)])


def exchange(messages, route, unpacked, empty):
    rounds, chips = len(messages), lax.axis_size("az") // 2
    blocks = {}
    for at in route[0]:
        pairs = [(2 * c + k, 2 * (c ^ partner(route, at, k)) + k) for c in range(chips) for k in range(2)]
        blocks[at, 0] = lax.ppermute(messages[rounds - 1 - at], "az", pairs)
    groups, state = arrivals(route), []
    for group in groups:
        fresh = [tag for tag in group if not tag[1]]
        if state:
            tied = lax.optimization_barrier(([blocks[tag] for tag in fresh], state))
            state = list(tied[1])
            blocks.update(zip(fresh, tied[0]))
        for at, _ in fresh:
            blocks[at, 1] = swap(blocks[at, 0])
        if group is not groups[-1]:
            state = list(unpacked(group, [blocks[tag] for tag in group], state, empty))
    return groups[-1], [blocks[tag] for tag in groups[-1]], state


def local(fields, cotangent, azimuth_filter, radial_filter, mixing, tap_offsets):
    size = lax.axis_size("az")
    rounds = size // 4
    near, rad, feat = fields.shape
    azim = near * size
    taps, rtaps, channels = tap_offsets.shape[0], radial_filter.shape[0], mixing.shape[0]
    many = rounds > 8
    first, second = plan(rounds)
    other_f, other_g = swap(fields), swap(cotangent)
    arguments = (fields, cotangent, azimuth_filter, radial_filter, mixing, tap_offsets)
    kept = [
        pltpu.VMEM(fields.shape, BF16),
        pltpu.VMEM(fields.shape, BF16),
        pltpu.VMEM((taps + rtaps, feat), F32),
        pltpu.VMEM((feat, feat), BF16),
        pltpu.SMEM((taps,), jnp.int32),
    ]
    fields, cotangent, filters, mix, tap_offsets = pl.pallas_call(
        gather,
        in_specs=[pl.BlockSpec(memory_space=pltpu.HBM)] * len(arguments),
        out_specs=[VMEM] * 4 + [SMEM],
        out_shape=kept,
        scratch_shapes=[
            pltpu.VMEM(azimuth_filter.shape, F32),
            pltpu.VMEM(radial_filter.shape, F32),
            pltpu.VMEM(mixing.shape, BF16),
            pltpu.SemaphoreType.DMA((len(arguments),)),
        ],
        compiler_params=PARAMS,
        name="gather",
    )(*(pltpu.with_memory_space_constraint(x, pltpu.HBM) for x in arguments))
    other_f, other_g, fields, cotangent = lax.optimization_barrier(
        (other_f, other_g, fields, cotangent)
    )
    body = 2 * near * ROWS
    length = 2 * body + HALO * 2 * near
    messages = call(
        functools.partial(pack, first),
        (fields, cotangent, other_f, other_g),
        [((length, feat), BF16)] * rounds,
        [((2 * near * (rad + 2 * ROWS), feat), F32), ((2 * near, rad, feat), F32)]
        + [((rounds, length, feat), BF16)] * many,
        name="pack",
    )

    def receiver(tags, blocks, state, empty):
        return call(
            functools.partial(receive_some, tags, first, taps, rtaps, len(state)),
            (filters, mix, *blocks, *state),
            empty,
            [],
            old=len(state),
            name="receive",
        )

    flat = ((azim * ROWS, feat), BF16)
    twice = ((2 * azim, ROWS, feat), F32)
    empty = [((azim * 2 * ROWS, feat), F32), twice, twice, flat]
    tags, blocks, state = exchange(messages, first, receiver, empty)
    sums = (taps + rtaps + channels) // 2 + 8
    messages = call(
        functools.partial(convolve, tags, first, second, taps, rtaps, channels, len(state)),
        (tap_offsets, filters, mix, *blocks, *state),
        [((2 * body + sums, feat), BF16)] * rounds,
        ([] if state else empty)
        + [flat, flat]
        + [((rounds, length, feat), BF16)] * many,
        name="convolve",
    )

    def collector(tags, blocks, state, empty):
        return call(
            functools.partial(collect_some, tags, second, len(state)),
            (*blocks, *state),
            empty,
            [],
            old=len(state),
            name="collect",
        )

    empty = [((near, rad, feat), F32), ((near, rad + 2 * ROWS, feat), F32), ((sums, feat), F32)]
    tags, blocks, state = exchange(messages, second, collector, empty)
    scale = 1.0 / math.sqrt(azim * rad * (feat // channels))
    ins = (fields, cotangent, filters, mix, *blocks, *state)
    outs = [
        (fields.shape, BF16),
        (fields.shape, BF16),
        ((taps, channels), F32),
        ((rtaps, channels), F32),
        ((channels, channels), F32),
    ]
    return pl.pallas_call(
        functools.partial(finish, tags, second, taps, rtaps, scale, len(state)),
        in_specs=[VMEM] * len(ins),
        out_specs=[pl.BlockSpec(memory_space=pltpu.HBM)] * len(outs),
        out_shape=[jax.ShapeDtypeStruct(*out) for out in outs],
        scratch_shapes=[pltpu.VMEM(*out) for out in ([] if state else empty) + outs]
        + [pltpu.SemaphoreType.DMA((len(outs),))]
        + [pltpu.VMEM((rounds, 2 * body + sums, feat), BF16)] * many,
        compiler_params=PARAMS,
        name="finish",
    )(*(pltpu.with_memory_space_constraint(x, pltpu.VMEM) for x in ins))


def solution(mesh):
    cells = P(("parts", "az"), None, None)
    parts = P("parts", None)
    return jax.shard_map(
        lambda *args: tuple(local(*args)),
        mesh=mesh,
        in_specs=(cells, cells, P(), P(), P(), P()),
        out_specs=(cells, cells, parts, parts, parts),
        check_vma=False,
    )
```

```python
import functools
import math

import jax
import jax.numpy as jnp
from jax import lax
from jax.experimental import pallas as pl
from jax.experimental.pallas import tpu as pltpu
from jax.sharding import PartitionSpec as P

F32, BF16 = jnp.float32, jnp.bfloat16
VMEM = pl.BlockSpec(memory_space=pltpu.VMEM)
SMEM = pl.BlockSpec(memory_space=pltpu.SMEM)
ROWS = 8
HALO = 3
SLAB = 8
PARAMS = pltpu.CompilerParams(vmem_limit_bytes=56 * 1024 * 1024)


def place():
    at = lax.axis_index("az")
    return at // 2, at % 2


def gather(field, cot, azimuth, radial, mixing, offsets, *refs):
    own_f, own_g, filters, mix, own_offsets, azimuth_in, radial_in, mixing_in, sems = refs
    pairs = (
        (azimuth, azimuth_in),
        (radial, radial_in),
        (mixing, mixing_in),
        (offsets, own_offsets),
        (field, own_f),
        (cot, own_g),
    )
    copies = [pltpu.make_async_copy(*pair, sems.at[i]) for i, pair in enumerate(pairs)]
    for copy in copies:
        copy.start()
    filters[...] = jnp.zeros(filters.shape, F32)
    mix[...] = jnp.zeros(mix.shape, BF16)
    for copy in copies[:3]:
        copy.wait()
    taps, channels = azimuth_in.shape
    rtaps, feat = radial_in.shape[0], mix.shape[0]
    for low in range(0, feat, channels):
        cell = slice(low, low + channels)
        filters[0:taps, cell] = azimuth_in[...]
        filters[taps : taps + rtaps, cell] = radial_in[...]
        mix[cell, cell] = mixing_in[...]
    for copy in copies[3:]:
        copy.wait()


def visit(refs, stage, step, fill=False):
    if stage is None:
        for i, ref in enumerate(refs):
            step(i, ref)
        return
    if not fill:
        for i, ref in enumerate(refs):
            stage[i] = ref[...]

    def body(i, carry):
        step(i, stage.at[i])
        return carry

    lax.fori_loop(0, len(refs), body, 0)
    if fill:
        for i, ref in enumerate(refs):
            ref[...] = stage[i]


def unpack(tags, refs, stage, core, take):
    if stage is None:
        for (at, swapped), ref in zip(tags, refs):
            take(at, core ^ swapped, ref)
        return
    half = len(refs) // 2
    for swapped in range(2):
        visit(
            refs[swapped * half : (swapped + 1) * half],
            stage,
            lambda i, ref, side=core ^ swapped: take(half - 1 - i, side, ref),
        )


def plan(rounds):
    if rounds == 4:
        return ((3, 1, 2, 0), (3,), 3), ((3, 1, 2, 0), (3, 1), 2)
    descending = tuple(reversed(range(rounds)))
    return (descending, (), 1), (descending, (), 1)


def partner(route, at, side):
    return 2 * at + (side ^ (at in route[1]) if isinstance(at, int) else side)


def arrivals(route):
    order = route[0]
    if len(order) != 4:
        return [[(at, swapped) for swapped in range(2) for at in order]]
    a, b, c, d = order
    if route[2] == 2:
        return [[(a, 0), (b, 0), (a, 1), (c, 0), (d, 0)], [(b, 1), (c, 1), (d, 1)]]
    return [[(a, 0), (b, 0)], [(c, 0), (d, 0), (a, 1), (b, 1)], [(c, 1), (d, 1)]]


def pack(route, own_f, own_g, other_f, other_g, *refs):
    rounds = len(route[0])
    outs, (fields, cots, *stage) = refs[:rounds], refs[rounds:]
    chip, core = place()
    near, rad, feat = own_f.shape
    step = rad + 2 * ROWS
    wide = fields.reshape(2 * near, step, feat)
    edge = jnp.zeros((2 * near, ROWS, feat), F32)
    wide[:, 0:ROWS, :] = edge
    wide[:, ROWS + rad : step, :] = edge
    for side, f, g in ((core, own_f, own_g), (1 - core, other_f, other_g)):
        wide[pl.ds(side * near, near), ROWS : ROWS + rad, :] = f[...].astype(F32)
        cots[pl.ds(side * near, near)] = g[...].astype(F32)
    body = 2 * near * ROWS

    half = feat // 2

    def beside(moved, kept, cell):
        lane = lax.broadcasted_iota(jnp.int32, moved.shape, 1)
        return jnp.where((lane < half) == (cell == 1), pltpu.roll(moved, half, 1), kept).astype(BF16)

    def fill(i, out):
        to = chip ^ partner(route, rounds - 1 - i, core)
        cell = to % 2
        first = to // 2 * (2 * ROWS)

        def rows(ref, start, second):
            start = pl.multiple_of(start + ROWS * second, ROWS)
            return ref[:, pl.ds(start, ROWS), :].reshape(body, feat)

        def pair(ref, start):
            return beside(rows(ref, start, 1 - cell), rows(ref, start, cell), cell)

        out[0:body, :] = pair(wide, first + ROWS)
        for h in range(HALO):
            at = body + h * 2 * near
            above, between = first + ROWS - HALO + h, HALO + 2 * ROWS
            out[at : at + 2 * near, :] = beside(
                fields[pl.ds(above + between * (1 - cell), 2 * near, stride=step), :],
                fields[pl.ds(above + between * cell, 2 * near, stride=step), :],
                cell,
            )
        at = body + HALO * 2 * near
        out[at : at + body, :] = pair(cots, first)

    visit(outs, stage[0] if stage else None, fill, fill=True)


def receive(tags, route, taps, rtaps, filters, mix, blocks, state, stage):
    fields, radial, grads, cots = state
    chip, core = place()
    rounds = len(route[0])
    azim, feat = radial.shape[0] // 2, mix.shape[0]
    step = 2 * ROWS
    wide = fields.reshape(azim, step, feat)
    near = azim // (2 * rounds)
    body = near * ROWS
    weight = [jnp.broadcast_to(filters[taps + j : taps + j + 1, :], (ROWS, feat)) for j in range(rtaps)]

    def take(at, side, block):
        first = (chip ^ partner(route, at, side)) * near
        wide[pl.ds(first, near), HALO : HALO + ROWS, :] = (
            block[0:body, :].astype(F32).reshape(near, ROWS, feat)
        )
        lane = lax.broadcasted_iota(jnp.int32, (near, feat), 1)
        for h in range(HALO):
            start = body + h * near
            edge = block[start : start + near, :].astype(F32)

            def row(r):
                return pl.ds(first * step + r, near, stride=step)

            lower = pltpu.roll(fields[row(ROWS + h), :], feat // 2, 1)
            upper = pltpu.roll(fields[row(HALO + h), :], feat // 2, 1)
            fields[row(h), :] = jnp.where(lane < feat // 2, edge, lower)
            fields[row(HALO + ROWS + h), :] = jnp.where(lane < feat // 2, upper, edge)
        start = body + HALO * near
        cot = block[start : start + body, :]
        cots[pl.ds(pl.multiple_of(first * ROWS, body), body), :] = cot
        back = lax.dot_general(cot, mix[...], (((1,), (1,)), ((), ())), preferred_element_type=F32)
        back = back.astype(BF16).astype(F32).reshape(near, ROWS, feat)
        grads[pl.ds(first, near)] = back
        grads[pl.ds(azim + first, near)] = back
        total = weight[0] * wide[pl.ds(first, near), 0:ROWS, :]
        for j in range(1, rtaps):
            total = total + weight[j] * wide[pl.ds(first, near), j : j + ROWS, :]
        radial[pl.ds(first, near)] = total
        radial[pl.ds(azim + first, near)] = total

    unpack(tags, blocks, stage[0] if stage else None, core, take)


def receive_some(tags, route, taps, rtaps, old, filters, mix, *refs):
    receive(tags, route, taps, rtaps, filters, mix, refs[: len(tags)], refs[len(tags) + old :], ())


def convolve(tags, route_in, route, taps, rtaps, channels, old, offsets, filters, mix, *refs):
    rounds = len(route[0])
    blocks, state = refs[: len(tags)], refs[len(tags) : len(tags) + old]
    outs, rest = refs[len(tags) + old :][:rounds], refs[len(tags) + old + rounds :]
    if not old:
        state, rest = rest[:4], rest[4:]
    hidden, spread, *stage = rest
    fields, radial, grads, cots = state
    receive(tags, route_in, taps, rtaps, filters, mix, blocks, state, stage)
    chip, core = place()
    azim, feat = radial.shape[0] // 2, mix.shape[0]
    wide = fields.reshape(azim, 2 * ROWS, feat)
    body = azim // (2 * rounds) * ROWS
    weight = [jnp.broadcast_to(filters[k : k + 1, :], (ROWS, feat)) for k in range(taps)]
    ahead = [lax.rem(offsets[k] + azim, azim) for k in range(taps)]
    behind = [lax.rem(azim - offsets[k], azim) for k in range(taps)]

    def slab(n, sums):
        sums = list(sums)
        a = n * SLAB
        grad = grads[pl.ds(a, SLAB)]
        value = jnp.zeros((SLAB, ROWS, feat), F32)
        back = jnp.zeros((SLAB, ROWS, feat), F32)
        for k in range(taps):
            x = radial[pl.ds(a + ahead[k], SLAB)]
            value = value + weight[k] * x
            sums[k] = sums[k] + jnp.sum(x * grad, axis=0)
            back = back + weight[k] * grads[pl.ds(a + behind[k], SLAB)]
        rows = pl.ds(pl.multiple_of(a * ROWS, SLAB * ROWS), SLAB * ROWS)
        hidden[rows, :] = value.reshape(SLAB * ROWS, feat).astype(BF16)
        spread[rows, :] = back.reshape(SLAB * ROWS, feat).astype(BF16)
        for j in range(rtaps):
            sums[taps + j] = sums[taps + j] + jnp.sum(
                wide[pl.ds(a, SLAB), j : j + ROWS, :] * back, axis=0
            )
        return tuple(sums)

    zero = jnp.zeros((ROWS, feat), F32)
    sums = lax.fori_loop(0, azim // SLAB, slab, (zero,) * (taps + rtaps), unroll=4)
    product = lax.dot_general(
        hidden[...], cots[...], (((0,), (0,)), ((), ())), preferred_element_type=F32
    )
    lane = lax.broadcasted_iota(jnp.int32, (channels, feat), 1)
    mixed = jnp.where(lane < channels, product[0:channels], product[channels:feat])
    part = jnp.concatenate([jnp.sum(s, axis=0, keepdims=True) for s in sums] + [mixed], axis=0)
    part = part + pltpu.roll(part, channels, 1)
    few, half = (taps + rtaps) // 2, channels // 2
    low = jnp.concatenate([part[0:few], part[2 * few : 2 * few + half]], axis=0)
    high = jnp.concatenate([part[few : 2 * few], part[2 * few + half : 2 * few + channels]], axis=0)
    lane = lax.broadcasted_iota(jnp.int32, low.shape, 1)
    part = jnp.where(lane < channels, low, high)
    part = jnp.concatenate([part, jnp.zeros((8, feat), F32)], axis=0).astype(BF16)
    for i, out in enumerate(outs):
        to = chip ^ partner(route, rounds - 1 - i, core)
        rows = pl.ds(pl.multiple_of(to * body, body), body)
        out[0:body, :] = hidden[rows, :]
        out[body : 2 * body, :] = spread[rows, :]
        out[2 * body : 2 * body + part.shape[0], :] = part


def collect(tags, route, blocks, state, stage):
    hidden, spread, summed = state
    chip, core = place()
    near, feat = hidden.shape[0], hidden.shape[2]
    body = near * ROWS
    mine = pl.multiple_of(core * body, body)

    half = feat // 2
    lane = lax.broadcasted_iota(jnp.int32, (body, feat), 1)

    def put(ref, start, value, cell):
        start = pl.multiple_of(start, ROWS)
        old = ref[:, pl.ds(start, ROWS), :].reshape(body, feat)
        new = jnp.where((lane >= half) == (cell == 1), value, old)
        ref[:, pl.ds(start, ROWS), :] = new.reshape(near, ROWS, feat)

    def take(at, side, block):
        source = chip ^ partner(route, at, side)
        first, cell = source // 2 * (2 * ROWS), source % 2
        for ref, start, edge in ((hidden, mine, 0), (spread, 2 * body + mine, ROWS)):
            value = block[pl.ds(start, body), :].astype(F32)
            put(ref, first + edge + ROWS * cell, value, cell)
            put(ref, first + edge + ROWS * (1 - cell), pltpu.roll(value, half, 1), cell)
        summed[...] += block[4 * body : 4 * body + summed.shape[0], :].astype(F32)

    unpack(tags, blocks, stage[0] if stage else None, core, take)


def clear(state):
    hidden, spread, summed = state
    near, rad, feat = hidden.shape
    spread[:, 0:ROWS, :] = jnp.zeros((near, ROWS, feat), F32)
    spread[:, ROWS + rad :, :] = jnp.zeros((near, ROWS, feat), F32)
    summed[...] = jnp.zeros(summed.shape, F32)


def collect_some(tags, route, old, *refs):
    state = refs[len(tags) + old :]
    if not old:
        clear(state)
    collect(tags, route, refs[: len(tags)], state, ())


def finish(tags, route, taps, rtaps, scale, old, field, cot, filters, mix, *refs):
    blocks, state = refs[: len(tags)], refs[len(tags) : len(tags) + old]
    targets, rest = refs[len(tags) + old :][:5], refs[len(tags) + old + 5 :]
    if not old:
        state, rest = rest[:3], rest[3:]
        clear(state)
    hidden, spread, summed = state
    out, grad, azimuth_out, radial_out, mixing_out, sems, *stage = rest
    collect(tags, route, blocks, state, stage)
    near, rad, feat = field.shape
    channels = azimuth_out.shape[1]
    sources = (out, grad, azimuth_out, radial_out, mixing_out)
    copies = [pltpu.make_async_copy(*pair, sems.at[i]) for i, pair in enumerate(zip(sources, targets))]
    flat = hidden[...].reshape(near * rad, feat).astype(BF16)
    mixed = jnp.dot(flat, mix[...], preferred_element_type=F32).reshape(near, rad, feat)
    out[...] = (field[...].astype(F32) + mixed).astype(BF16)
    copies[0].start()
    total = jnp.zeros((near, rad, feat), F32)
    for j in range(rtaps):
        weight = jnp.broadcast_to(filters[taps + j : taps + j + 1, :], (rad, feat))
        first = ROWS + HALO - j
        total = total + weight * spread[:, first : first + rad, :]
    branch = total.astype(BF16).astype(F32)
    grad[...] = (cot[...].astype(F32) + branch).astype(BF16)
    copies[1].start()
    few, half = (taps + rtaps) // 2, channels // 2
    part = summed[0 : few + half, :] * scale
    azimuth_out[0:few, :] = part[0:few, 0:channels]
    azimuth_out[few:taps, :] = part[0 : taps - few, channels:feat]
    radial_out[...] = part[taps - few : few, channels:feat]
    mixing_out[0:half, :] = part[few : few + half, 0:channels]
    mixing_out[half:channels, :] = part[few : few + half, channels:feat]
    for copy in copies[2:]:
        copy.start()
    for copy in copies:
        copy.wait()


def call(kernel, ins, outs, scratch, old=0, name=None):
    ins = [
        pltpu.with_memory_space_constraint(x, pltpu.VMEM if x.ndim > 1 else pltpu.SMEM) for x in ins
    ]
    return pl.pallas_call(
        kernel,
        in_specs=[VMEM if x.ndim > 1 else SMEM for x in ins],
        out_specs=[VMEM] * len(outs),
        out_shape=[pltpu.VMEM(*out) for out in outs],
        scratch_shapes=[pltpu.VMEM(*out) for out in scratch],
        input_output_aliases={len(ins) - old + i: i for i in range(old)},
        compiler_params=PARAMS,
        name=name,
    )(*ins)


def swap(x):
    size = lax.axis_size("az")
    return lax.ppermute(x, "az", [(i, i ^ 1) for i in range(size)])


def exchange(messages, route, unpacked, empty):
    rounds, chips = len(messages), lax.axis_size("az") // 2
    blocks = {}
    for at in route[0]:
        pairs = [(2 * c + k, 2 * (c ^ partner(route, at, k)) + k) for c in range(chips) for k in range(2)]
        blocks[at, 0] = lax.ppermute(messages[rounds - 1 - at], "az", pairs)
    groups, state = arrivals(route), []
    for group in groups:
        fresh = [tag for tag in group if not tag[1]]
        if state:
            tied = lax.optimization_barrier(([blocks[tag] for tag in fresh], state))
            state = list(tied[1])
            blocks.update(zip(fresh, tied[0]))
        for at, _ in fresh:
            blocks[at, 1] = swap(blocks[at, 0])
        if group is not groups[-1]:
            state = list(unpacked(group, [blocks[tag] for tag in group], state, empty))
    return groups[-1], [blocks[tag] for tag in groups[-1]], state


def local(fields, cotangent, azimuth_filter, radial_filter, mixing, tap_offsets):
    size = lax.axis_size("az")
    rounds = size // 4
    near, rad, feat = fields.shape
    azim = near * size
    taps, rtaps, channels = tap_offsets.shape[0], radial_filter.shape[0], mixing.shape[0]
    many = rounds > 8
    first, second = plan(rounds)
    other_f, other_g = swap(fields), swap(cotangent)
    arguments = (fields, cotangent, azimuth_filter, radial_filter, mixing, tap_offsets)
    kept = [
        pltpu.VMEM(fields.shape, BF16),
        pltpu.VMEM(fields.shape, BF16),
        pltpu.VMEM((taps + rtaps, feat), F32),
        pltpu.VMEM((feat, feat), BF16),
        pltpu.SMEM((taps,), jnp.int32),
    ]
    fields, cotangent, filters, mix, tap_offsets = pl.pallas_call(
        gather,
        in_specs=[pl.BlockSpec(memory_space=pltpu.HBM)] * len(arguments),
        out_specs=[VMEM] * 4 + [SMEM],
        out_shape=kept,
        scratch_shapes=[
            pltpu.VMEM(azimuth_filter.shape, F32),
            pltpu.VMEM(radial_filter.shape, F32),
            pltpu.VMEM(mixing.shape, BF16),
            pltpu.SemaphoreType.DMA((len(arguments),)),
        ],
        compiler_params=PARAMS,
        name="gather",
    )(*(pltpu.with_memory_space_constraint(x, pltpu.HBM) for x in arguments))
    other_f, other_g, fields, cotangent = lax.optimization_barrier(
        (other_f, other_g, fields, cotangent)
    )
    body = 2 * near * ROWS
    length = 2 * body + HALO * 2 * near
    messages = call(
        functools.partial(pack, first),
        (fields, cotangent, other_f, other_g),
        [((length, feat), BF16)] * rounds,
        [((2 * near * (rad + 2 * ROWS), feat), F32), ((2 * near, rad, feat), F32)]
        + [((rounds, length, feat), BF16)] * many,
        name="pack",
    )

    def receiver(tags, blocks, state, empty):
        return call(
            functools.partial(receive_some, tags, first, taps, rtaps, len(state)),
            (filters, mix, *blocks, *state),
            empty,
            [],
            old=len(state),
            name="receive",
        )

    flat = ((azim * ROWS, feat), BF16)
    twice = ((2 * azim, ROWS, feat), F32)
    empty = [((azim * 2 * ROWS, feat), F32), twice, twice, flat]
    tags, blocks, state = exchange(messages, first, receiver, empty)
    sums = (taps + rtaps + channels) // 2 + 8
    messages = call(
        functools.partial(convolve, tags, first, second, taps, rtaps, channels, len(state)),
        (tap_offsets, filters, mix, *blocks, *state),
        [((2 * body + sums, feat), BF16)] * rounds,
        ([] if state else empty)
        + [flat, flat]
        + [((rounds, length, feat), BF16)] * many,
        name="convolve",
    )

    def collector(tags, blocks, state, empty):
        return call(
            functools.partial(collect_some, tags, second, len(state)),
            (*blocks, *state),
            empty,
            [],
            old=len(state),
            name="collect",
        )

    empty = [((near, rad, feat), F32), ((near, rad + 2 * ROWS, feat), F32), ((sums, feat), F32)]
    tags, blocks, state = exchange(messages, second, collector, empty)
    scale = 1.0 / math.sqrt(azim * rad * (feat // channels))
    ins = (fields, cotangent, filters, mix, *blocks, *state)
    outs = [
        (fields.shape, BF16),
        (fields.shape, BF16),
        ((taps, channels), F32),
        ((rtaps, channels), F32),
        ((channels, channels), F32),
    ]
    return pl.pallas_call(
        functools.partial(finish, tags, second, taps, rtaps, scale, len(state)),
        in_specs=[VMEM] * len(ins),
        out_specs=[pl.BlockSpec(memory_space=pltpu.HBM)] * len(outs),
        out_shape=[jax.ShapeDtypeStruct(*out) for out in outs],
        scratch_shapes=[pltpu.VMEM(*out) for out in ([] if state else empty) + outs]
        + [pltpu.SemaphoreType.DMA((len(outs),))]
        + [pltpu.VMEM((rounds, 2 * body + sums, feat), BF16)] * many,
        compiler_params=PARAMS,
        name="finish",
    )(*(pltpu.with_memory_space_constraint(x, pltpu.VMEM) for x in ins))


def solution(mesh):
    cells = P(("parts", "az"), None, None)
    parts = P("parts", None)
    return jax.shard_map(
        lambda *args: tuple(local(*args)),
        mesh=mesh,
        in_specs=(cells, cells, P(), P(), P(), P()),
        out_specs=(cells, cells, parts, parts, parts),
        check_vma=False,
    )
```
